32 devices in a mesh: dp: 16 (over z, y, x), feat: 2 (over core).
Axes of the slice: x: 2, y: 2, z: 4, core: 2. Of those that a mesh axis runs over, the one named last changes fastest.
Arguments:
- inputs: float32 [20480, 640], P('dp', 'feat'), may hold values from -6 to 6
- encoder: bfloat16 [20480, 640], P('dp', 'feat'), may hold values from -6 to 6
- output_grad: float32 [20480, 640], P('dp', 'feat'), may hold values from -6 to 6
- target_lengths: int32 [32, 24], P(('dp', 'feat')), may hold values from 0 to 256, as said below
- source_lengths: int32 [32, 24], P(('dp', 'feat')), may hold values from 0 to 256, as said below
- gains: float32 [3, 640], P(None, 'feat'), may hold values from 0.5 to 1.5
- shifts: float32 [3, 640], P(None, 'feat'), may hold values from -2 to 2
- self_inproj: bfloat16 [640, 1920], replicated, may hold values from -0.25 to 0.25
- self_outproj: bfloat16 [640, 640], replicated, may hold values from -1 to 1
- cross_query: bfloat16 [640, 640], replicated, may hold values from -0.25 to 0.25
- cross_keyvalue: bfloat16 [640, 1280], replicated, may hold values from -0.25 to 0.25
- cross_outproj: bfloat16 [640, 640], replicated, may hold values from -1 to 1
- ffn_expand: bfloat16 [640, 3072], replicated, may hold values from -0.25 to 0.25
- ffn_reduce: bfloat16 [3072, 640], replicated, may hold values from -0.109375 to 0.109375
Outputs:
- layer_out: float32 [20480, 640], P('dp', 'feat')
- input_grad: float32 [20480, 640], P('dp', 'feat')
- encoder_grad: float32 [20480, 640], P('dp', 'feat')
- gain_grad: float32 [3, 640], P(None, 'feat')
- shift_grad: float32 [3, 640], P(None, 'feat')
- self_inproj_grad: float32 [640, 1920], P('dp', 'feat')
- self_outproj_grad: float32 [640, 640], P('dp', 'feat')
- cross_query_grad: float32 [640, 640], P('dp', 'feat')
- cross_keyvalue_grad: float32 [640, 1280], P('dp', 'feat')
- cross_outproj_grad: float32 [640, 640], P('dp', 'feat')
- ffn_expand_grad: float32 [640, 3072], P('dp', 'feat')
- ffn_reduce_grad: float32 [3072, 640], P('dp', 'feat')
The draws below stay inside these ranges and needn't reach their ends.
Inputs may be any that keep to these rules, and one draw needn't show every extreme that they name: `target_lengths`: in each bucket the nonzero lengths fill the first slots and zeros the rest; a bucket's lengths sum to 640 or less; in every draw one bucket, chosen from the seed, has a first sentence of 256. `source_lengths`: nonzero exactly where target_lengths is, and at most the target length.
All inputs are finite; a program needn't handle non-finite values.
Results may differ from the reference program's by a relative error of at most 0.017.
Values may be sent and summed in bfloat16 or wider, within the bound.
A program may use at most 192 MiB of HBM per device.

```python
import math
import jax
import jax.numpy as jnp
from jax import lax

D = 640
HEADS = 8
FF = 3072
ROWS = 640
SENTS = 24
SHORT = 40
MAXLEN = 256
BUCKETS = 32
TOKENS = 20480


def length_pair(key):
    base = jax.random.fold_in(key, 7331)
    keys = jax.random.split(base, 5)
    short = jax.random.randint(keys[0], (BUCKETS, SENTS), 1, SHORT + 1)
    long_len = jax.random.randint(keys[1], (BUCKETS, SENTS), SHORT + 1, MAXLEN + 1)
    pick = jax.random.randint(keys[2], (BUCKETS, SENTS), 0, 8)
    lengths = jnp.where(pick == 0, long_len, short)
    chosen = jax.random.randint(keys[3], (), 0, BUCKETS)
    first = (jnp.arange(BUCKETS) == chosen)[:, None] & (jnp.arange(SENTS) == 0)[None, :]
    lengths = jnp.where(first, MAXLEN, lengths)
    ends = jnp.cumsum(lengths, axis=1)
    lengths = jnp.where(ends <= ROWS, lengths, 0)
    raw_cut = jax.random.randint(keys[4], (BUCKETS, SENTS), 0, 1 << 20)
    cut = raw_cut % (lengths // 4 + 1)
    source = jnp.where(first, MAXLEN, lengths - cut)
    return (lengths.astype(jnp.int32), source.astype(jnp.int32))


def draw_target_lengths(key, part):
    return length_pair(key)[0]


def draw_source_lengths(key, part):
    return length_pair(key)[1]


def level_of(rng, extent, cuts, least, top_value):
    factor_of, own = 1.0, jax.random.fold_in(rng, 6)
    for dim, blocks in cuts:
        heights = jnp.exp(jax.random.uniform(jax.random.fold_in(own, dim), (blocks,), jnp.float32, least / len(cuts), top_value / len(cuts)))
        factor_of = factor_of * jnp.repeat(heights, extent[dim] // blocks).reshape([-1 if axis == dim else 1 for axis in range(len(extent))])
    return factor_of


def scatter_about(own_key, extent, scale, most, cuts=(), kind=jnp.bfloat16):
    drawn = jax.random.normal(own_key, extent, jnp.float32) * scale
    if len(cuts) > 0:
        drawn = level_of(own_key, extent, cuts, -0.22, 0.18) * drawn
    return jnp.clip(drawn, min=-most, max=most).astype(kind)


def setup_inputs(seed: int = 0) -> dict:
    key_of = jax.random.split(jax.random.key(seed), 15)
    return {
        "inputs": scatter_about(key_of[0], (TOKENS, D), 1.0, 6.0, ((0, 16), (1, 2)), jnp.float32),
        "encoder": scatter_about(key_of[1], (TOKENS, D), 1.0, 6.0, ((0, 16), (1, 2))),
        "output_grad": scatter_about(key_of[2], (TOKENS, D), 1.0, 6.0, ((0, 16), (1, 2)), jnp.float32),
        "target_lengths": draw_target_lengths(jax.random.fold_in(key_of[14], 71), 0),
        "source_lengths": draw_source_lengths(jax.random.fold_in(key_of[14], 71), 0),
        "gains": jnp.clip(1.0 + 0.1 * jax.random.normal(key_of[5], (3, D), jnp.float32), 0.5, 1.5),
        "shifts": scatter_about(key_of[6], (3, D), 0.5, 2.0, ((1, 2),), jnp.float32),
        "self_inproj": scatter_about(key_of[7], (D, 3 * D), D ** -0.5, 0.25),
        "self_outproj": scatter_about(key_of[8], (D, D), (D // 16) ** -0.5, 1.0),
        "cross_query": scatter_about(key_of[9], (D, D), D ** -0.5, 0.25),
        "cross_keyvalue": scatter_about(key_of[10], (D, 2 * D), D ** -0.5, 0.25),
        "cross_outproj": scatter_about(key_of[11], (D, D), (D // 16) ** -0.5, 1.0),
        "ffn_expand": scatter_about(key_of[12], (D, FF), D ** -0.5, 0.25),
        "ffn_reduce": scatter_about(key_of[13], (FF, D), FF ** -0.5, 0.109375),
    }


HIGHEST = lax.Precision.HIGHEST
EPSILON = 1e-05
MASKED_SCORE = -1e+30

@jax.custom_vjp
def low(v):
    return lax.optimization_barrier(v.astype(jnp.bfloat16)).astype(jnp.float32)

@jax.custom_vjp
def low_back(v):
    return v

def low_keep(v):
    return (low(v), None)

def low_pass(kept, grad):
    return (grad,)

def back_keep(v):
    return (v, None)

def back_low(kept, grad):
    return (low(grad),)
low.defvjp(low_keep, low_pass)
low_back.defvjp(back_keep, back_low)

def matmul(left, right):
    return jnp.dot(left, right, precision=HIGHEST, preferred_element_type=jnp.float32)

def smooth_gate(values):
    return jax.nn.gelu(values, approximate=True)

def layer_norm(values, gain, shift):
    center = lax.optimization_barrier(jnp.mean(values, axis=-1, keepdims=True))
    second = lax.optimization_barrier(jnp.mean(values * values, axis=-1, keepdims=True))
    return (values - center) * lax.rsqrt(second - center * center + EPSILON) * gain + shift

def sentence_rows(lengths, count):
    ends = jnp.cumsum(lengths.astype(jnp.int32), dtype=jnp.int32).astype(jnp.int32)
    positions = jnp.arange(count, dtype=jnp.int32)
    sentence = lax.optimization_barrier(jnp.sum((ends[None, :] <= positions[:, None]).astype(jnp.int32), axis=1, dtype=jnp.int32)).astype(jnp.int32)
    return (sentence, positions < ends[-1])

def attention(queries, keys, values, allowed):
    count = queries.shape[0]
    width = queries.shape[1]
    head_size = width // HEADS
    q_heads = queries.reshape(count, HEADS, head_size)
    k_heads = keys.reshape(keys.shape[0], HEADS, head_size)
    v_heads = values.reshape(values.shape[0], HEADS, head_size)
    scores = jnp.einsum('qhd,khd->hqk', q_heads, k_heads, precision=HIGHEST) * (1.0 / math.sqrt(head_size))
    scores = low_back(scores)
    scores = jnp.where(allowed[None, :, :], scores, jnp.asarray(MASKED_SCORE, scores.dtype))
    weights = jax.nn.softmax(scores, axis=-1)
    mixed = jnp.einsum('hqk,khd->qhd', low(weights), v_heads, precision=HIGHEST)
    return low_back(low(mixed.reshape(count, width)))

def block(rows_in, rows_enc, lengths_t, lengths_s, gains, shifts, self_inproj, self_outproj, cross_query, cross_keyvalue, cross_outproj, ffn_expand, ffn_reduce):
    count = rows_in.shape[0]
    width = rows_in.shape[1]
    target_seg, target_valid = sentence_rows(lengths_t, count)
    source_seg, source_valid = sentence_rows(lengths_s, rows_enc.shape[0])
    positions = jnp.arange(count, dtype=jnp.int32)
    keep = jnp.where(target_valid, 1.0, 0.0).astype(rows_in.dtype)[:, None]
    self_mask = (target_seg[:, None] == target_seg[None, :]) & (positions[None, :] <= positions[:, None])
    self_mask = self_mask & target_valid[:, None] & target_valid[None, :]
    cross_mask = (target_seg[:, None] == source_seg[None, :]) & target_valid[:, None] & source_valid[None, :]
    normed1 = low_back(low(layer_norm(rows_in, gains[0], shifts[0])))
    projected = low_back(low(matmul(normed1, self_inproj)))
    queries = projected[:, :width]
    keys = projected[:, width:2 * width]
    values = projected[:, 2 * width:]
    attended1 = attention(queries, keys, values, self_mask)
    mid1 = rows_in + low_back(low(matmul(attended1, self_outproj) * keep))
    normed2 = low_back(low(layer_norm(mid1, gains[1], shifts[1])))
    cross_queries = low_back(low(matmul(normed2, cross_query)))
    source = low_back(rows_enc)
    memory = low_back(low(matmul(source, cross_keyvalue)))
    attended2 = attention(cross_queries, memory[:, :width], memory[:, width:], cross_mask)
    mid2 = mid1 + low_back(low(matmul(attended2, cross_outproj) * keep))
    normed3 = low_back(low(layer_norm(mid2, gains[2], shifts[2])))
    expanded = low_back(low(matmul(normed3, ffn_expand)))
    activated = low(smooth_gate(expanded))
    reduced = matmul(activated, ffn_reduce)
    return mid2 + low_back(low(reduced * keep))

def reference(inputs, encoder, output_grad, target_lengths, source_lengths, gains, shifts, self_inproj, self_outproj, cross_query, cross_keyvalue, cross_outproj, ffn_expand, ffn_reduce):
    buckets = target_lengths.shape[0]
    width = inputs.shape[1]

    def forward(rows_all, enc_all, gain_all, shift_all, *weights):

        def one(item):
            rows_in, rows_enc, lengths_t, lengths_s = item
            return jax.checkpoint(block)(rows_in, rows_enc, lengths_t, lengths_s, gain_all, shift_all, *weights)
        outputs = lax.map(one, (rows_all.reshape(buckets, -1, width), enc_all.reshape(buckets, -1, width), target_lengths.astype(jnp.int32), source_lengths.astype(jnp.int32)))
        return outputs.reshape(rows_all.shape)
    weights = [w.astype(jnp.float32) for w in (self_inproj, self_outproj, cross_query, cross_keyvalue, cross_outproj, ffn_expand, ffn_reduce)]
    layer_out, pull = jax.vjp(forward, inputs, encoder.astype(jnp.float32), gains, shifts, *weights)
    grads = pull(output_grad)
    return (layer_out, grads[0], grads[1], grads[2], grads[3], grads[4], grads[5], grads[6], grads[7], grads[8], grads[9], grads[10])
```

```python
import math

import jax
import jax.numpy as jnp
from jax import lax
from jax.sharding import PartitionSpec as P

HEADS = 8


EPSILON = 1e-05
MASKED_SCORE = -1e30


def as_sent(array):

    def short(part):
        return part.astype(jnp.bfloat16) if part.dtype == jnp.float32 else part

    return jax.tree.map(short, array)


def inner(left, right):
    return lax.dot_general(
        left, right, (((0,), (0,)), ((), ())), preferred_element_type=jnp.float32
    )


def backward_product(grad, weight):
    return lax.dot_general(
        grad, weight, (((1,), (1,)), ((), ())), preferred_element_type=jnp.float32
    )


def smooth_gate(values):
    return jax.nn.gelu(values, approximate=True)


def row_sums(first, second):
    return (first, second)


def to_tokens(parts):
    return parts


def to_features(parts):
    return parts


def gather_rows(part):
    return lax.all_to_all(part, "feat", split_axis=0, concat_axis=1, tiled=True)


def spread_rows(part):
    return lax.all_to_all(part, "feat", split_axis=1, concat_axis=0, tiled=True)


def norm_forward(values, gain, shift):
    width = values.shape[1]
    total, squares = row_sums(jnp.sum(values, axis=1), jnp.sum(values * values, axis=1))
    center = total / width
    reciprocal = lax.rsqrt(squares / width - center * center + EPSILON)
    normed = (values - center[:, None]) * reciprocal[:, None]
    return (normed, reciprocal, (normed * gain + shift).astype(jnp.bfloat16))


def norm_backward(grad_normed, normed, reciprocal, gain):
    width = normed.shape[1]
    grad_value = grad_normed.astype(jnp.float32)
    scaled = grad_value * gain
    first, second = row_sums(jnp.sum(scaled, axis=1), jnp.sum(scaled * normed, axis=1))
    grad_input = reciprocal[:, None] * (
        scaled - first[:, None] / width - normed * (second[:, None] / width)
    )
    return (grad_input, jnp.sum(grad_value * normed, axis=0), jnp.sum(grad_value, axis=0))


def sentence_rows(lengths, count):
    slots = jnp.arange(lengths.shape[1], dtype=jnp.int32)
    ends = jnp.sum(
        jnp.where(slots[:, None] <= slots[None, :], lengths[0][:, None], 0), axis=0, dtype=jnp.int32
    )
    positions = jnp.arange(count, dtype=jnp.int32)
    sentence = jnp.sum(
        (ends[None, :] <= positions[:, None]).astype(jnp.int32), axis=1, dtype=jnp.int32
    )
    return (sentence, positions < ends[-1])


def split_heads(values):
    return values.reshape(values.shape[0], HEADS, values.shape[1] // HEADS)


def head_scores(queries, keys, allowed):
    head_size = queries.shape[1] // HEADS
    scores = jnp.einsum(
        "qhd,khd->hqk", split_heads(queries), split_heads(keys), preferred_element_type=jnp.float32
    ) * (1.0 / math.sqrt(head_size))
    return jnp.where(allowed[None, :, :], scores, MASKED_SCORE)


def attend_forward(queries, keys, values, allowed):
    scores = head_scores(queries, keys, allowed)
    largest = jnp.max(scores, axis=-1, keepdims=True)
    expo = jnp.exp(scores - largest)
    total = jnp.sum(expo, axis=-1, keepdims=True)
    weights = expo / total
    mixed = jnp.einsum(
        "hqk,khd->qhd",
        weights.astype(jnp.bfloat16),
        split_heads(values),
        preferred_element_type=jnp.float32,
    )
    log_total = largest[..., 0] + jnp.log(total[..., 0])
    return (mixed.reshape(queries.shape).astype(jnp.bfloat16), log_total)


def attend_backward(queries, keys, values, allowed, log_total, grad_mixed):
    head_size = queries.shape[1] // HEADS
    scale = 1.0 / math.sqrt(head_size)
    weights = jnp.exp(head_scores(queries, keys, allowed) - log_total[..., None])
    grad_heads = split_heads(grad_mixed)
    grad_weights = jnp.einsum(
        "qhd,khd->hqk", grad_heads, split_heads(values), preferred_element_type=jnp.float32
    )
    grad_values = jnp.einsum(
        "hqk,qhd->khd", weights.astype(jnp.bfloat16), grad_heads, preferred_element_type=jnp.float32
    )
    centre = jnp.sum(weights * grad_weights, axis=-1, keepdims=True)
    grad_scores = (weights * (grad_weights - centre)).astype(jnp.bfloat16)
    grad_queries = (
        jnp.einsum(
            "hqk,khd->qhd", grad_scores, split_heads(keys), preferred_element_type=jnp.float32
        )
        * scale
    )
    grad_keys = (
        jnp.einsum(
            "hqk,qhd->khd", grad_scores, split_heads(queries), preferred_element_type=jnp.float32
        )
        * scale
    )
    return (
        grad_queries.reshape(queries.shape),
        grad_keys.reshape(keys.shape),
        grad_values.reshape(values.shape),
    )


def masked_rows(grad, valid):
    return jnp.where(valid[:, None], grad, jnp.zeros_like(grad))


def per_device(
    inputs,
    encoder,
    output_grad,
    target_lengths,
    source_lengths,
    gains,
    shifts,
    self_inproj,
    self_outproj,
    cross_query,
    cross_keyvalue,
    cross_outproj,
    ffn_expand,
    ffn_reduce,
):
    inputs = gather_rows(inputs)
    encoder = gather_rows(encoder)
    output_grad = gather_rows(output_grad)
    gains = lax.all_gather(gains, "feat", axis=1, tiled=True)
    shifts = lax.all_gather(shifts, "feat", axis=1, tiled=True)
    count = inputs.shape[0]
    width = self_outproj.shape[0]
    target_seg, target_valid = sentence_rows(target_lengths, count)
    source_seg, source_valid = sentence_rows(source_lengths, count)
    positions = jnp.arange(count, dtype=jnp.int32)
    keep = target_valid.astype(jnp.float32)[:, None]
    self_mask = (target_seg[:, None] == target_seg[None, :]) & (
        positions[None, :] <= positions[:, None]
    )
    self_mask = self_mask & target_valid[:, None] & target_valid[None, :]
    cross_mask = (
        (target_seg[:, None] == source_seg[None, :]) & target_valid[:, None] & source_valid[None, :]
    )
    normed_one, recip_one, normed_cols = norm_forward(inputs, gains[0], shifts[0])
    (normed1,) = to_tokens((normed_cols,))
    projected = jnp.dot(normed1, self_inproj, preferred_element_type=jnp.float32).astype(
        jnp.bfloat16
    )
    queries = projected[:, :width]
    keys = projected[:, width : 2 * width]
    values = projected[:, 2 * width :]
    attended1, log_one = attend_forward(queries, keys, values, self_mask)
    branch = (jnp.dot(attended1, self_outproj, preferred_element_type=jnp.float32) * keep).astype(
        jnp.bfloat16
    )
    (branch_cols,) = to_features((branch,))
    mid_one = inputs + branch_cols.astype(jnp.float32)
    normed_two, recip_two, normed_cols = norm_forward(mid_one, gains[1], shifts[1])
    normed2, source_rows = to_tokens((normed_cols, encoder))
    cross_queries = jnp.dot(normed2, cross_query, preferred_element_type=jnp.float32).astype(
        jnp.bfloat16
    )
    memory = jnp.dot(source_rows, cross_keyvalue, preferred_element_type=jnp.float32).astype(
        jnp.bfloat16
    )
    attended2, log_two = attend_forward(
        cross_queries, memory[:, :width], memory[:, width:], cross_mask
    )
    branch = (jnp.dot(attended2, cross_outproj, preferred_element_type=jnp.float32) * keep).astype(
        jnp.bfloat16
    )
    (branch_cols,) = to_features((branch,))
    mid_two = mid_one + branch_cols.astype(jnp.float32)
    normed_three, recip_three, normed_cols = norm_forward(mid_two, gains[2], shifts[2])
    (normed3,) = to_tokens((normed_cols,))
    expanded = jnp.dot(normed3, ffn_expand, preferred_element_type=jnp.float32).astype(jnp.bfloat16)
    gated, gate_pull = jax.vjp(smooth_gate, expanded.astype(jnp.float32))
    activated = gated.astype(jnp.bfloat16)
    branch = (jnp.dot(activated, ffn_reduce, preferred_element_type=jnp.float32) * keep).astype(
        jnp.bfloat16
    )
    (branch_cols,) = to_features((branch,))
    layer_out = mid_two + branch_cols.astype(jnp.float32)
    (grad_branch,) = to_tokens((output_grad.astype(jnp.bfloat16),))
    grad_branch = masked_rows(grad_branch, target_valid)
    reduce_grad = inner(activated, grad_branch)
    grad_act = backward_product(grad_branch, ffn_reduce)
    (grad_pre,) = gate_pull(grad_act)
    grad_expanded = grad_pre.astype(jnp.bfloat16)
    expand_grad = inner(normed3, grad_expanded)
    grad_normed = backward_product(grad_expanded, ffn_expand).astype(jnp.bfloat16)
    (grad_cols,) = to_features((grad_normed,))
    part_three, gain_three, shift_three = norm_backward(
        grad_cols, normed_three, recip_three, gains[2]
    )
    grad_mid_two = output_grad + part_three
    (grad_branch,) = to_tokens((grad_mid_two.astype(jnp.bfloat16),))
    grad_branch = masked_rows(grad_branch, target_valid)
    cross_out_grad = inner(attended2, grad_branch)
    grad_attended = backward_product(grad_branch, cross_outproj).astype(jnp.bfloat16)
    grad_cq, grad_ck, grad_cv = attend_backward(
        cross_queries, memory[:, :width], memory[:, width:], cross_mask, log_two, grad_attended
    )
    grad_cq = grad_cq.astype(jnp.bfloat16)
    grad_memory = jnp.concatenate([grad_ck, grad_cv], axis=1).astype(jnp.bfloat16)
    cross_query_grad = inner(normed2, grad_cq)
    cross_kv_grad = inner(source_rows, grad_memory)
    grad_normed = backward_product(grad_cq, cross_query).astype(jnp.bfloat16)
    grad_source = backward_product(grad_memory, cross_keyvalue).astype(jnp.bfloat16)
    grad_cols, grad_source_cols = to_features((grad_normed, grad_source))
    part_two, gain_two, shift_two = norm_backward(grad_cols, normed_two, recip_two, gains[1])
    grad_mid_one = grad_mid_two + part_two
    (grad_branch,) = to_tokens((grad_mid_one.astype(jnp.bfloat16),))
    grad_branch = masked_rows(grad_branch, target_valid)
    self_out_grad = inner(attended1, grad_branch)
    grad_attended = backward_product(grad_branch, self_outproj).astype(jnp.bfloat16)
    grad_q, grad_k, grad_v = attend_backward(
        queries, keys, values, self_mask, log_one, grad_attended
    )
    grad_projected = jnp.concatenate([grad_q, grad_k, grad_v], axis=1).astype(jnp.bfloat16)
    self_in_grad = inner(normed1, grad_projected)
    grad_normed = backward_product(grad_projected, self_inproj).astype(jnp.bfloat16)
    (grad_cols,) = to_features((grad_normed,))
    part_one, gain_one, shift_one = norm_backward(grad_cols, normed_one, recip_one, gains[0])
    input_grad = grad_mid_one + part_one
    gain_local = jnp.stack([gain_one, gain_two, gain_three], axis=0)
    shift_local = jnp.stack([shift_one, shift_two, shift_three], axis=0)
    vectors = lax.psum(jnp.concatenate([gain_local, shift_local], axis=0), ("dp", "feat"))
    half = vectors.shape[1] // lax.axis_size("feat")
    vectors = lax.dynamic_slice_in_dim(vectors, lax.axis_index("feat") * half, half, axis=1)
    gain_grad, shift_grad = vectors[:3], vectors[3:]
    weight_terms = (
        self_in_grad,
        self_out_grad,
        cross_query_grad,
        cross_kv_grad,
        cross_out_grad,
        expand_grad,
        reduce_grad,
    )
    summed = []
    for term in weight_terms:
        pair = lax.psum_scatter(
            term.astype(jnp.bfloat16), "feat", scatter_dimension=1, tiled=True
        )
        summed.append(
            lax.psum_scatter(pair, "dp", scatter_dimension=0, tiled=True).astype(jnp.float32)
        )
    return (
        spread_rows(layer_out),
        spread_rows(input_grad),
        spread_rows(grad_source_cols).astype(jnp.float32),
        gain_grad,
        shift_grad,
        *summed,
    )


def solution(mesh):
    in_specs = (
        P("dp", "feat"),
        P("dp", "feat"),
        P("dp", "feat"),
        P(("dp", "feat"), None),
        P(("dp", "feat"), None),
        P(None, "feat"),
        P(None, "feat"),
        P(),
        P(),
        P(),
        P(),
        P(),
        P(),
        P(),
    )
    out_specs = (
        P("dp", "feat"),
        P("dp", "feat"),
        P("dp", "feat"),
        P(None, "feat"),
        P(None, "feat"),
        P("dp", "feat"),
        P("dp", "feat"),
        P("dp", "feat"),
        P("dp", "feat"),
        P("dp", "feat"),
        P("dp", "feat"),
        P("dp", "feat"),
    )
    return jax.shard_map(
        per_device, mesh=mesh, in_specs=in_specs, out_specs=out_specs, check_vma=False
    )
```

```python
import functools
import math

import jax
import jax.numpy as jnp
from jax import lax
from jax.experimental import pallas as pl
from jax.experimental.pallas import tpu as pltpu
from jax.sharding import PartitionSpec as P

HEADS = 8
LONGEST = 256
EPSILON = 1e-05
MASKED = -1e30
F32 = jnp.float32
BF16 = jnp.bfloat16
WINDOW = 256
HIDDEN_TILE = 256
W_IN, W_OUT, W_CQ, W_KV, W_CO, W_EXPAND, W_REDUCE, W_IN_AGAIN = range(8)
FFN, FFN_END, NORM_3, CROSS_START, CROSS, MIXED, KV, NORM_2, SELF_START, SELF, IN, NORM_1, END = range(13)
EXPAND0, EXPAND1, EXPAND2, REDUCE0, REDUCE1, S_MIX, S_KV, S_OUT, S_IN0, S_IN1, S_IN2 = PIECES = range(11)
EXPANDS, REDUCES = (EXPAND0, EXPAND1, EXPAND2), (REDUCE0, REDUCE1)
FEAT, X, Y, Z1, Z2 = range(5)
QUERY_BLOCKS = ((0, 256), (256, 256), (512, 128))
VMEM_LIMIT = 63 * 2**20


def nn(left, right):
    return lax.dot_general(left, right, (((1,), (0,)), ((), ())), preferred_element_type=F32)


def nt(left, right):
    return lax.dot_general(left, right, (((1,), (1,)), ((), ())), preferred_element_type=F32)


def self_blocks(rows):
    found = []
    for start, size in QUERY_BLOCKS:
        first = max(0, start - LONGEST)
        found.append((start, size, first, start + size - first))
    return found


def cross_blocks(rows):
    return [(start, size, 0, min(rows, start + size + LONGEST)) for start, size in QUERY_BLOCKS]


def gelu_parts(value):
    root = math.sqrt(2.0 / math.pi)
    square = value * value
    inner = value * (root + (root * 0.044715) * square)
    bent = jnp.tanh(inner)
    up = 0.5 + 0.5 * bent
    slope = (0.5 * value) * (1.0 - bent * bent) * (root + (3.0 * root * 0.044715) * square)
    return value * up, up + slope


def norm_stats(value):
    mean = jnp.mean(value, axis=1, keepdims=True)
    second = jnp.mean(value * value, axis=1, keepdims=True)
    scale = lax.rsqrt(second - mean * mean + EPSILON)
    return (value - mean) * scale, scale


def pack_halves(left, right):
    width = left.shape[1]
    low = lax.broadcasted_iota(jnp.int32, left.shape, 1) < width // 2
    return (
        jnp.where(low, left, pltpu.roll(right, width // 2, 1)),
        jnp.where(low, pltpu.roll(left, width // 2, 1), right),
    )


def in_spans(width):
    half, part = 3 * width // 2, 384
    high = half + 64
    yield S_IN0, ((0, part), (high, part))
    yield S_IN1, ((part, part), (high + part, part))
    yield S_IN2, ((2 * part, 256), (high + 2 * part, 128))


class Layer:
    def __init__(self, **refs):
        self.__dict__.update(refs)
        self.rows, self.width = self.normed1.shape
        self.hidden = self.w_expand.shape[1]
        self.head = self.width // HEADS
        most = -(-self.rows // 256) * 128
        self.halves = [(0, most), (most, self.rows - most)]


    def segments(self, lengths, shape, axis):
        place = lax.broadcasted_iota(jnp.int32, shape, axis)
        found = jnp.zeros(shape, jnp.int32)
        end = jnp.int32(0)
        for slot in range(lengths.shape[1]):
            end = end + lengths[0, slot]
            found = found + jnp.where(place >= end, 1, 0)
        return found, place < end, place

    def prepare(self):
        rows = self.rows
        seg, valid, _ = self.segments(self.t_len, (rows, 128), 0)
        self.keep[...] = jnp.where(valid, 1.0, 0.0).astype(F32)
        self.t_col[...] = jnp.where(valid, seg, -2)
        seg, valid, _ = self.segments(self.s_len, (rows, 128), 0)
        self.s_col[...] = jnp.where(valid, seg, -2)
        seg, valid, _ = self.segments(self.t_len, (8, rows), 1)
        self.t_row[...] = jnp.where(valid, seg, -1)

    def make_bias(self, blocks, column, causal):
        for ref, (q0, qn, k0, kn) in zip(self.bias, blocks):
            allowed = column[k0 : k0 + kn, 0:1] == self.t_row[0:1, q0 : q0 + qn]
            if causal:
                key = lax.broadcasted_iota(jnp.int32, (kn, qn), 0) + k0
                query = lax.broadcasted_iota(jnp.int32, (kn, qn), 1) + q0
                allowed = allowed & (key <= query)
            ref[0:kn, :] = jnp.where(allowed, 0.0, MASKED).astype(F32)


    def window(self, head):
        tiles = jnp.minimum((head * self.head) // 128, (self.width - WINDOW) // 128)
        start = pl.multiple_of(tiles * 128, 128)
        lane = lax.broadcasted_iota(jnp.int32, (8, WINDOW), 1) + start
        mine = (lane >= head * self.head) & (lane < (head + 1) * self.head)
        return start, jnp.where(mine, 1.0, 0.0).astype(F32)[0:1]

    def attend(self, queries, q_at, keys, k_at, mixed_t, blocks):
        factor = math.log2(math.e) / math.sqrt(self.head)

        @pl.loop(0, HEADS)
        def _(head):
            start, mine = self.window(head)
            band = pl.ds(pl.multiple_of(head * self.head, 16), self.head)
            for b, (q0, qn, k0, kn) in enumerate(blocks):
                query = queries[q0 : q0 + qn, pl.ds(q_at + start, WINDOW)]
                query = (query.astype(F32) * mine).astype(BF16)
                key = keys[k0 : k0 + kn, pl.ds(k_at + start, WINDOW)]
                scores = nt(key, query) + self.bias[b][0:kn, :]
                largest = jnp.max(scores, axis=0, keepdims=True)
                expo = jnp.exp2((scores - largest) * factor)
                total = jnp.sum(expo, axis=0, keepdims=True)
                weights = (expo * (1.0 / total)).astype(BF16)
                self.p[b][head, 0:kn, :] = weights
                mixed = nn(self.v_t[band, k0 : k0 + kn], weights)
                mixed_t[band, q0 : q0 + qn] = mixed.astype(BF16)

    def attend_back(self, queries, q_at, keys, k_at, values, v_at, mixed_t, blocks, name):
        scale = 1.0 / math.sqrt(self.head)
        self.dk[...] = jnp.zeros(self.dk.shape, F32)
        self.dv[...] = jnp.zeros(self.dv.shape, F32)

        @pl.loop(0, HEADS)
        def _(head):
            start, mine = self.window(head)
            band = pl.ds(pl.multiple_of(head * self.head, 16), self.head)
            lanes = pl.ds(start, WINDOW)
            for b, (q0, qn, k0, kn) in enumerate(blocks):
                query = queries[q0 : q0 + qn, pl.ds(q_at + start, WINDOW)]
                query = (query.astype(F32) * mine).astype(BF16)
                grad = (self.g[q0 : q0 + qn, lanes].astype(F32) * mine).astype(BF16)
                value = values[k0 : k0 + kn, pl.ds(v_at + start, WINDOW)]
                weights = self.p[b][head, 0:kn, :]
                product = self.g_t[band, q0 : q0 + qn].astype(F32) * mixed_t[band, q0 : q0 + qn].astype(F32)
                centre = jnp.sum(product, axis=0, keepdims=True)
                grad_w = nt(value, grad)
                grad_s = (weights.astype(F32) * (grad_w - centre)).astype(BF16)
                self.dv[k0 : k0 + kn, lanes] += nn(weights, grad)
                self.dk[k0 : k0 + kn, lanes] += nn(grad_s, query)
                grad_q = nn(self.k_t[band, k0 : k0 + kn], grad_s)
                self.dq_t[band, q0 : q0 + qn] = (grad_q * scale).astype(BF16)
            self.tick(name, head)


    def norm_to(self, value, which, start, size, target):
        normed, _ = norm_stats(value)
        gain, shift = self.gs[which : which + 1, :], self.gs[3 + which : 4 + which, :]
        target[start : start + size, :] = (normed * gain + shift).astype(BF16)

    def norm_back(self, grad, value, which, first):
        normed, scale = norm_stats(value)
        scaled = grad * self.gs[which : which + 1, :]
        one = jnp.mean(scaled, axis=1, keepdims=True)
        two = jnp.mean(scaled * normed, axis=1, keepdims=True)
        gain = jnp.sum(grad * normed, axis=0, keepdims=True)
        shift = jnp.sum(grad, axis=0, keepdims=True)
        if first:
            self.vec[which : which + 1, :] = gain
            self.vec[3 + which : 4 + which, :] = shift
        else:
            self.vec[which : which + 1, :] += gain
            self.vec[3 + which : 4 + which, :] += shift
        return (scaled - one - normed * two) * scale


    def forward_self(self):
        width = self.width
        for start, size in self.halves:
            part = slice(start, start + size)
            self.norm_to(self.x[part, :], 0, start, size, self.normed1)
        self.arrive(W_IN)
        for col in range(0, 3 * width, width):
            self.proj[:, col : col + width] = nn(
                self.normed1[...], self.w_in[:, col : col + width]
            ).astype(BF16)
        self.v_t[...] = self.proj[:, 2 * width :].T
        self.make_bias(self_blocks(self.rows), self.t_col, True)
        self.attend(self.proj, 0, self.proj, width, self.mixed1_t, self_blocks(self.rows))

    def forward_cross(self):
        width = self.width
        self.spill_weights()
        self.arrive(W_KV)
        enc = self.encoder_rows(self.k_t)
        for col in range(0, 2 * width, width):
            self.memory[:, col : col + width] = nn(
                enc[...], self.w_kv[:, col : col + width]
            ).astype(BF16)
        self.v_t[...] = self.memory[:, width:].T
        self.g[...] = self.mixed1_t[...].T
        self.arrive(W_OUT)
        self.arrive(W_CQ)
        for start, size in self.halves:
            part = slice(start, start + size)
            branch = (nn(self.g[part, :], self.w_out[...]) * self.keep[part, 0:1]).astype(BF16)
            mid = self.x[part, :] + branch.astype(F32)
            self.mid1[part, :] = mid
            self.norm_to(mid, 1, start, size, self.normed2)
            self.cq[part, :] = nn(self.normed2[part, :], self.w_cq[...]).astype(BF16)
        self.make_bias(cross_blocks(self.rows), self.s_col, False)
        self.spill_wait()
        self.attend(self.cq, 0, self.memory, 0, self.mixed2_t, cross_blocks(self.rows))

    def feed_forward(self):
        width, tile = self.width, HIDDEN_TILE
        self.g[...] = self.mixed2_t[...].T
        self.arrive(W_CO)
        for start, size in self.halves:
            part = slice(start, start + size)
            branch = (nn(self.g[part, :], self.w_co[...]) * self.keep[part, 0:1]).astype(BF16)
            mid = self.mid1[part, :] + branch.astype(F32)
            self.mid2[part, :] = mid
            self.norm_to(mid, 2, start, size, self.normed3)
        self.k_t[...] = self.normed3[...].T
        self.landed(2)
        for start, size in self.halves:
            part = slice(start, start + size)
            self.g[part, :] = (self.grad_rows(part) * self.keep[part, 0:1]).astype(BF16)
        self.dk[...] = jnp.zeros(self.dk.shape, F32)
        self.dv[...] = jnp.zeros(self.dv.shape, F32)
        self.arrive(W_EXPAND)
        self.arrive(W_REDUCE)

        @pl.loop(0, self.hidden // (2 * tile))
        def _(step):
            reduced = []
            low = pl.multiple_of(step * tile, tile)
            for side in range(2):
                at = pl.multiple_of(side * (self.hidden // 2) + step * tile, tile)
                expand = self.w_expand[:, pl.ds(at, tile)]
                reduce = self.w_reduce[pl.ds(at, tile), :]
                value = nn(self.normed3[...], expand).astype(BF16).astype(F32)
                active, slope = gelu_parts(value)
                active = active.astype(BF16)
                grad = (nt(self.g[...], reduce) * slope).astype(BF16)
                self.dk[...] += nn(active, reduce)
                self.dv[...] += nt(grad, expand)
                self.put_expand(step, side, low, nn(self.k_t[...], grad))
                reduced.append(nn(active.T, self.g[...]))
            for side, packed in enumerate(pack_halves(*reduced)):
                self.put_reduce(step, side, low, packed)
            self.tick(FFN, step)

        self.tick(FFN_END)
        for n, (start, size) in enumerate(self.halves):
            part = slice(start, start + size)
            mid = self.mid2[part, :]
            branch = (self.dk[part, :] * self.keep[part, 0:1]).astype(BF16)
            self.put_layer_out(part, mid + branch.astype(F32))
            grad = self.dv[part, :].astype(BF16).astype(F32)
            self.mid2[part, :] = self.grad_rows(part) + self.norm_back(grad, mid, 2, n == 0)
        self.tick(NORM_3)

    def backward_cross(self):
        width = self.width
        self.mid_grad[...] = (self.mid2[...] * self.keep[:, 0:1]).astype(BF16)
        self.g[...] = nt(self.mid_grad[...], self.w_co[...]).astype(BF16)
        self.g_t[...] = self.g[...].T
        self.k_t[...] = self.memory[:, 0:width].T
        self.tick(CROSS_START)
        self.attend_back(
            self.cq, 0, self.memory, 0, self.memory, width, self.mixed2_t, cross_blocks(self.rows), CROSS
        )
        self.refetch()
        out_grad = nn(self.mixed2_t[...], self.mid_grad[...])
        self.fetch_weights()
        scale = 1.0 / math.sqrt(self.head)
        self.gmem[:, 0:width] = (self.dk[...] * scale).astype(BF16)
        self.gmem[:, width : 2 * width] = self.dv[...].astype(BF16)
        self.g[...] = self.dq_t[...].T
        self.k_t[...] = self.normed2[...].T
        for side, packed in enumerate(pack_halves(out_grad, nn(self.k_t[...], self.g[...]))):
            self.put_rows(S_MIX, side, packed)
        self.tick(MIXED)
        enc_t = self.encoder_columns(self.k_t)
        for side in range(2):
            self.put_rows(
                S_KV, side, nn(enc_t[...], self.gmem[:, side * width : (side + 1) * width])
            )
        self.tick(KV)
        for n, (start, size) in enumerate(self.halves):
            part = slice(start, start + size)
            self.put_encoder_grad(part, nt(self.gmem[part, 0 : 2 * width], self.w_kv[...]).astype(BF16))
            grad = nt(self.g[part, :], self.w_cq[...]).astype(BF16).astype(F32)
            self.mid2[part, :] += self.norm_back(grad, self.mid1[part, :], 1, n == 0)
        self.tick(NORM_2)

    def backward_self(self):
        width = self.width
        self.mid_grad[...] = (self.mid2[...] * self.keep[:, 0:1]).astype(BF16)
        self.g[...] = nt(self.mid_grad[...], self.w_out[...]).astype(BF16)
        self.g_t[...] = self.g[...].T
        self.k_t[...] = self.proj[:, width : 2 * width].T
        self.put_rows_split(S_OUT, nn(self.mixed1_t[...], self.mid_grad[...]))
        self.fetch_wait()
        self.tick(SELF_START)
        self.attend_back(
            self.proj, 0, self.proj, width, self.proj, 2 * width, self.mixed1_t, self_blocks(self.rows), SELF
        )
        scale = 1.0 / math.sqrt(self.head)
        self.gmem[:, 0:width] = self.dq_t[...].T
        self.gmem[:, width : 2 * width] = (self.dk[...] * scale).astype(BF16)
        self.gmem[:, 2 * width :] = self.dv[...].astype(BF16)
        self.k_t[...] = self.normed1[...].T
        for n, (name, spans) in enumerate(in_spans(width)):
            for side, (col, size) in enumerate(spans):
                value = nn(self.k_t[...], self.gmem[:, col : col + size])
                if n == 2 and side == 1:
                    odd = nn(self.k_t[...], self.gmem[:, 896:1024])
                    value = jnp.concatenate([value, pltpu.roll(odd, 64, 1)], axis=1)
                self.put_rows(name, side, value)
            self.tick(IN, n)
        self.arrive(W_IN_AGAIN)
        for n, (start, size) in enumerate(self.halves):
            part = slice(start, start + size)
            grad = nt(self.gmem[part, :], self.w_in[...]).astype(BF16).astype(F32)
            self.put_input_grad(
                part, self.mid2[part, :] + self.norm_back(grad, self.x[part, :], 0, n == 0)
            )
            self.tick(NORM_1, n)


def scratch_of(rows, width, hidden):
    wide = [k[3] for k in cross_blocks(rows)]
    vm = pltpu.VMEM
    named = dict(
        w_in=vm((width, 3 * width), BF16),
        w_out=vm((width, width), BF16),
        w_cq=vm((width, width), BF16),
        w_kv=vm((width, 2 * width), BF16),
        w_co=vm((width, width), BF16),
        w_expand=vm((width, hidden), BF16),
        w_reduce=vm((hidden, width), BF16),
        keep=vm((rows, 128), F32),
        t_col=vm((rows, 128), jnp.int32),
        s_col=vm((rows, 128), jnp.int32),
        t_row=vm((8, rows), jnp.int32),
        normed1=vm((rows, width), BF16),
        proj=vm((rows, 3 * width), BF16),
        v_t=vm((width, rows), BF16),
        mixed1_t=vm((width, rows), BF16),
        mid1=vm((rows, width), F32),
        pair=vm((2, rows, width), BF16),
        normed3=vm((rows, width), BF16),
        g=vm((rows, width), BF16),
        k_t=vm((width, rows), BF16),
        dk=vm((rows, width), F32),
        dv=vm((rows, width), F32),
        w_sem=pltpu.SemaphoreType.DMA((7,)),
        p_sem=pltpu.SemaphoreType.DMA((3,)),
        again_sem=pltpu.SemaphoreType.DMA(()),
    )
    for b, (_, qn, _, kn) in enumerate(cross_blocks(rows)):
        named[f"p{b}"] = vm((HEADS, kn, qn), BF16)
    return named


class SavedLayer(Layer):
    def put_rows_split(self, name, value):
        turned = pltpu.roll(value, value.shape[1] // 2, 1)
        for side, part in enumerate((value, turned)):
            self.put_rows(name, side, part[:, : LANES[name]])

    def start_weights(self):
        targets = (self.w_in, self.w_out, self.w_cq, self.w_kv, self.w_co, self.w_expand, self.w_reduce)
        self.copies = {
            n: pltpu.make_async_copy(self.sources[n], target, self.w_sem.at[n])
            for n, target in enumerate(targets)
        }
        for copy in self.copies.values():
            copy.start()

    def refetch(self):
        self.copies[W_IN_AGAIN] = pltpu.make_async_copy(
            self.sources[W_IN], self.w_in, self.again_sem
        )
        self.copies[W_IN_AGAIN].start()

    def arrive(self, name):
        self.copies[name].wait()

    def spill_copies(self, back):
        found = []
        for b, (_, _, _, kn) in enumerate(self_blocks(self.rows)):
            here, there = self.p[b].at[:, 0:kn, :], self.spill[b]
            pair = (there, here) if back else (here, there)
            found.append(pltpu.make_async_copy(*pair, self.p_sem.at[b]))
        return found

    def spill_weights(self):
        for copy in self.spill_copies(False):
            copy.start()

    def spill_wait(self):
        for copy in self.spill_copies(False):
            copy.wait()

    def fetch_weights(self):
        for copy in self.spill_copies(True):
            copy.start()

    def fetch_wait(self):
        for copy in self.spill_copies(True):
            copy.wait()

    def phases(self):
        self.forward_self()
        self.forward_cross()
        self.feed_forward()
        self.backward_cross()
        self.backward_self()


def share(p0, p1, p2, spill0, spill1, spill2, sources, pair, **named):
    rows, width = named["normed1"].shape
    first, expand, reduce, proj = (named[n] for n in ("w_in", "w_expand", "w_reduce", "proj"))

    def place(name, side):
        if name in (S_KV, S_MIX):
            at = side * width + (2 * width if name == S_MIX else 0)
            return reduce, pl.multiple_of(at, width), 0
        if name == S_OUT:
            return pair.at[side], 0, 0
        if name == S_IN2:
            return expand, 0, pl.multiple_of(4 * width + side * 256, 128)
        at = side * 768 + (384 if name == S_IN1 else 0)
        return proj, 0, pl.multiple_of(at, 128)

    return dict(
        named,
        g_t=named["v_t"],
        dq_t=named["normed3"],
        memory=first.at[:, 0 : 2 * width],
        cq=first.at[:, 2 * width : 3 * width],
        gmem=expand.at[:, 0 : 3 * width],
        mid_grad=expand.at[:, 3 * width : 4 * width],
        bias=[named["dk"].at[0:kn, q0 : q0 + qn] for q0, qn, _, kn in cross_blocks(rows)],
        p=(p0, p1, p2),
        spill=(spill0, spill1, spill2),
        sources=sources,
        normed2=pair.at[0],
        mixed2_t=pair.at[1],
        place=place,
    )


LANES = {S_MIX: 640, S_KV: 640, S_OUT: 384, S_IN0: 384, S_IN1: 384, S_IN2: 256}


class LocalLayer(SavedLayer):
    def staged(self, names):
        targets = {S_KV: self.to_kv, S_MIX: self.to_mix, S_OUT: self.to_out}
        targets.update({S_IN0: self.to_in0, S_IN1: self.to_in1, S_IN2: self.to_in2})
        found = []
        for name in names:
            for side in range(2):
                base, row, col = self.place(name, side)
                found.append(
                    pltpu.make_async_copy(
                        base.at[pl.ds(row, self.width), pl.ds(col, LANES[name])],
                        targets[name].at[side],
                        self.s_sem.at[2 * (name - S_MIX) + side],
                    )
                )
        return found

    def tick(self, name, step=None):
        for when, pieces in ((KV, (S_MIX, S_KV)), (SELF_START, (S_OUT,)), (NORM_1, (S_IN0, S_IN1, S_IN2))):
            if name == when and step in (None, 0):
                for copy in self.staged(pieces):
                    copy.start()

    def encoder_columns(self, spare):
        spare[...] = self.enc[...].T
        return spare

    def encoder_rows(self, spare):
        return self.enc

    def landed(self, n):
        pass

    def grad_rows(self, part):
        return self.og[part, :]

    def put_rows(self, name, side, value):
        base, row, col = self.place(name, side)
        base[pl.ds(row, self.width), pl.ds(col, value.shape[1])] = value.astype(BF16)

    def put_expand(self, step, side, low, value):
        self.s_expand[side, :, pl.ds(low, value.shape[1])] = value.astype(BF16)

    def put_reduce(self, step, side, low, value):
        self.s_reduce[side, pl.ds(low, value.shape[0]), :] = value.astype(BF16)

    def put_layer_out(self, part, value):
        self.layer_out[part, :] = value

    def put_input_grad(self, part, value):
        self.mid2[part, :] = value

    def put_encoder_grad(self, part, value):
        self.encoder_grad[part, :] = value

    def run(self):
        self.start_weights()
        self.prepare()
        self.vec[...] = jnp.zeros(self.vec.shape, F32)
        self.phases()
        for copy in self.staged((S_MIX, S_KV, S_OUT, S_IN0, S_IN1, S_IN2)):
            copy.wait()


MESH = pl.DeviceIdType.MESH
LAYER_OUT, ENCODER_GRAD, INPUT_GRAD = range(3)
SEND, FREE, BEGIN, REUSE = range(5, 9)
ORDER = {
    EXPAND0: (Z1, X, Y),
    EXPAND1: (Z1, Y, X),
    EXPAND2: (X, Y, Z1),
    REDUCE0: (Y, X, Z1),
    REDUCE1: (X, Y, Z1),
    S_MIX: (Y, X, Z1),
    S_KV: (X, Y, Z1),
    S_OUT: (Z1, Y, X),
    S_IN0: (X, Y, Z1),
    S_IN1: (Y, X, Z1),
    S_IN2: (Z1, X, Y),
}


class RemoteLayer(SavedLayer):
    def where_am_i(self):
        self.dp, self.feat = lax.axis_index("dp"), lax.axis_index("feat")
        bits = [lax.rem(lax.div(self.dp, 1 << n), 2) for n in range(4)]
        self.bit = dict(zip((X, Y, Z1, Z2), bits))
        self.peer = {FEAT: (self.dp, 1 - self.feat)}
        for n, link in enumerate((X, Y, Z1, Z2)):
            self.peer[link] = (self.dp + (1 << n) * (1 - 2 * bits[n]), self.feat)

    def remote(self, source, target, send, receive, link):
        return pltpu.make_async_remote_copy(
            source, target, send, receive, device_id=self.peer[link], device_id_type=MESH
        )

    def greet(self):
        barrier = pltpu.get_barrier_semaphore()
        for link in range(5):
            pl.semaphore_signal(barrier, 1, device_id=self.peer[link], device_id_type=MESH)
        pl.semaphore_wait(barrier, 5)


    def mine(self, size):
        return pl.ds(pl.multiple_of(self.feat * size, size), size)

    def other(self, size):
        return pl.ds(pl.multiple_of((1 - self.feat) * size, size), size)

    def exchange(self):
        rows, half = self.rows, self.width // 2
        pairs = ((self.x_in, self.x_t), (self.e_in, self.e_t), (self.g_in, self.grad_t))
        self.own, self.sent = [], []
        for n, (source, target) in enumerate(pairs):
            place = target.at[self.mine(half), :]
            mine, other = source.at[:, self.mine(rows)], source.at[:, self.other(rows)]
            self.own.append(pltpu.make_async_copy(mine, place, self.in_own.at[n]))
            self.sent.append(self.remote(other, place, self.in_send.at[n], self.in_recv.at[n], FEAT))
        place = self.gs_half.at[self.feat]
        self.sent.append(self.remote(place, place, self.in_send.at[3], self.in_recv.at[3], FEAT))

    def landed(self, n):
        if n < 3:
            self.own[n].wait()
        self.sent[n].wait()

    def encoder_rows(self, spare):
        self.landed(1)
        spare[...] = self.e_t[...].T
        return spare

    def encoder_columns(self, spare):
        return self.e_t

    def grad_rows(self, part):
        return self.grad_t[:, part].T


    def copies_out(self, name, local=True):
        source = self.grad_t if name == ENCODER_GRAD else self.x_t
        half = self.width // 2
        place = (self.layer_out, self.encoder_grad, self.input_grad)[name].at[:, self.mine(self.rows)]
        far = self.remote(
            source.at[self.other(half), :], place, self.out_send.at[name], self.out_recv.at[name], FEAT
        )
        if not local:
            return (far,)
        near = pltpu.make_async_copy(source.at[self.mine(half), :], place, self.out_own.at[name])
        return near, far

    def put_layer_out(self, part, value):
        self.x_t[:, part] = value.T

    def put_encoder_grad(self, part, value):
        self.grad_t[:, part] = value.astype(F32).T

    def put_input_grad(self, part, value):
        self.x_t[:, part] = value.T


    def spot(self, name, side, row, count):
        if name in EXPANDS:
            lanes = pl.ds(2 * HIDDEN_TILE * (name - EXPAND0), 2 * HIDDEN_TILE)
            return self.s_expand.at[side, pl.ds(row, count), lanes]
        if name in REDUCES:
            height = self.s_reduce.shape[1] // 2
            return self.s_reduce.at[side, pl.ds((name - REDUCE0) * height + row, count), :]
        base, top, left = self.place(name, side)
        return base.at[pl.ds(top + row, count), pl.ds(left, LANES[name])]

    def landing(self, name, side, row, count):
        if name in EXPANDS:
            lanes = pl.ds(2 * HIDDEN_TILE * (name - EXPAND0), 2 * HIDDEN_TILE)
            return self.l_expand.at[pl.ds(row, count), lanes]
        if name in REDUCES:
            height = self.s_reduce.shape[1] // 2
            return self.l_reduce.at[pl.ds((name - REDUCE0) * height + row, count), :]
        if name in (S_KV, S_MIX):
            first = self.width if name == S_MIX else 0
            return self.s_reduce.at[side, pl.ds(first + row, count), :]
        return self.s_expand.at[side, pl.ds(row, count), pl.ds(384 * (name - S_OUT), LANES[name])]

    def plan(self, name):
        quarter = (self.s_reduce.shape[1] // 2 if name in REDUCES else self.width) // 4
        links = ORDER[name]
        one = self.bit[links[0]] * 2 * quarter
        two = one + self.bit[links[1]] * quarter
        three = two + self.bit[links[2]] * (quarter // 2)
        return quarter, links, (one, two, three)

    def travel(self, name, step):
        n = name
        quarter, links, (one, two, _) = self.plan(name)
        here, there = self.feat, 1 - self.feat
        if step == 0:
            link, count = FEAT, 4 * quarter
            source = self.spot(name, there, 0, count)
            target = self.landing(name, here, 0, count)
        elif step == 1:
            link, count = links[0], 2 * quarter
            source = self.spot(name, here, (1 - self.bit[link]) * count, count)
            target = self.landing(name, there, 0, count)
        elif step == 2:
            link, count = links[1], quarter
            source = self.spot(name, here, one + (1 - self.bit[link]) * count, count)
            target = self.landing(name, there, 2 * quarter, count)
        elif step == 3:
            link, count = links[2], quarter // 2
            source = self.spot(name, here, two + (1 - self.bit[link]) * count, count)
            target = self.landing(name, there, 3 * quarter, count)
        else:
            link, source, target = Z2, self.z_send[n], self.z_land[n]
        return self.remote(source, target, self.send_sem.at[n, step], self.recv_sem.at[n, step], link)

    def credit_at(self, name, link):
        return self.credit.at[name, link]

    def allow(self, name, link):
        pl.semaphore_signal(self.credit_at(name, link), 1, device_id=self.peer[link], device_id_type=MESH)

    def go(self, name, step):
        link = (FEAT, *ORDER[name], Z2)[step]
        if step in (1, 2, 3) or (step == 0 and name >= S_MIX):
            pl.semaphore_wait(self.credit_at(name, link), 1)
        self.travel(name, step).start()

    def add(self, name, row, count, from_row):
        mine = self.spot(name, self.feat, row, count)
        mine[...] = mine[...] + self.landing(name, 1 - self.feat, from_row, count)[...]

    def step(self, name, step):
        n = name
        quarter, links, (one, two, three) = self.plan(name)
        self.travel(name, step).wait_recv()
        if step == 0:
            out = (1 - self.bit[links[0]]) * 2 * quarter
            for at in (out, out + quarter):
                self.add(name, at, quarter, at)
            for at in (one, one + quarter):
                self.add(name, at, quarter, at)
            for link in (X, Y, Z1):
                self.allow(name, link)
            self.go(name, 1)
        elif step == 1:
            out, kept = (1 - self.bit[links[1]]) * quarter, self.bit[links[1]] * quarter
            self.add(name, one + out, quarter, out)
            self.go(name, 2)
            self.add(name, one + kept, quarter, kept)
        elif step == 2:
            half = quarter // 2
            out, kept = (1 - self.bit[links[2]]) * half, self.bit[links[2]] * half
            self.add(name, two + out, half, 2 * quarter + out)
            self.go(name, 3)
            self.add(name, two + kept, half, 2 * quarter + kept)
        elif step == 3:
            half = quarter // 2
            value = self.spot(name, self.feat, three, half)[...].astype(F32)
            value = value + self.landing(name, 1 - self.feat, 3 * quarter, half)[...].astype(F32)
            if name in REDUCES:
                wide = self.width // 2
                low, high = value[:, :wide], pltpu.roll(value, wide, 1)[:, :wide]
            else:
                low, high = value[: half // 2], value[half // 2 :]
            first = self.bit[Z2] == 0
            self.z_keep[n][...] = jnp.where(first, low, high)
            self.z_send[n][...] = jnp.where(first, high, low).astype(BF16)
            self.go(name, 4)
        else:
            value = self.z_keep[n][...] + self.z_land[n][...].astype(F32)
            self.finish(name, value)

    def finish(self, name, value):
        half = self.width // 2
        if name in EXPANDS:
            at = 2 * HIDDEN_TILE * (name - EXPAND0)
            self.o_expand[:, at : at + value.shape[1]] = value
        elif name in REDUCES:
            at = value.shape[0] * (name - REDUCE0)
            self.o_reduce[at : at + value.shape[0], :] = value
        elif name == S_KV:
            self.o_kv[...] = value
        elif name == S_MIX:
            self.o_co[...] = value[:, :half]
            self.o_cq[...] = pltpu.roll(value, half, 1)[:, :half]
        elif name == S_OUT:
            self.o_out[...] = value[:, :half]
        elif name != S_IN2:
            self.z_keep[name][...] = value
        else:
            parts = [self.z_keep[S_IN0][...], self.z_keep[S_IN1][...], value]
            wide = jnp.concatenate(parts, axis=1)
            lane = lax.broadcasted_iota(jnp.int32, wide.shape, 1)
            moved = pltpu.roll(wide, 64, 1)
            moved = jnp.where(lane < 64, pltpu.roll(wide, 1024 - 896, 1), moved)
            self.o_in[...] = jnp.where(self.feat == 0, wide, moved)[:, : 3 * half]

    def seat(self, name, block):
        bits = {Z1: block // 4, Y: block // 2 % 2, X: block % 2}
        a, b, c = (bits[link] for link in ORDER[name])
        return 4 * a + 2 * b + c

    def in_pairs(self, value):
        rows = value.shape[0] // 16
        for n in range(8):
            part = [value[at * rows : (at + 1) * rows] for at in (n, n + 8)]
            yield n, jnp.concatenate(part, axis=0).astype(BF16)

    def put_rows(self, name, side, value):
        base, top, left = self.place(name, side)
        for block, part in self.in_pairs(value):
            row, count = self.seat(name, block) * part.shape[0], part.shape[0]
            base[pl.ds(top + row, count), pl.ds(left, part.shape[1])] = part

    def put_expand(self, step, side, low, value):
        which = lax.div(step, 2)
        for block, part in self.in_pairs(value):
            seats = [self.seat(name, block) for name in EXPANDS]
            seat = jnp.where(which == 0, seats[0], jnp.where(which == 1, seats[1], seats[2]))
            at = pl.multiple_of(seat * part.shape[0], 16)
            self.s_expand[side, pl.ds(at, part.shape[0]), pl.ds(low, value.shape[1])] = part

    def put_reduce(self, step, side, low, value):
        count, piece = 32, self.s_reduce.shape[1] // 2
        eighth = piece // 8
        for n in range(value.shape[0] // count):
            row = step * value.shape[0] + n * count
            block, rest = lax.div(row, 2 * eighth), lax.rem(row, 2 * eighth)
            bits = {Z1: lax.div(block, 4), Y: lax.rem(lax.div(block, 2), 2), X: lax.rem(block, 2)}
            which, inside = lax.div(rest, eighth), lax.rem(rest, eighth)
            seats = []
            for name in REDUCES:
                a, b, c = (bits[link] for link in ORDER[name])
                seats.append(4 * a + 2 * b + c)
            at = which * piece + jnp.where(which == 0, *seats) * eighth + inside
            part = value[n * count : (n + 1) * count].astype(BF16)
            self.s_reduce[side, pl.ds(pl.multiple_of(at, 32), count), :] = part


    def vec_go(self, step):
        n = len(PIECES)
        source = self.v_half.at[1 - self.feat] if step == 0 else self.v_sum.at[step - 1]
        self.remote(
            source, self.v_land.at[step], self.send_sem.at[n, step], self.recv_sem.at[n, step], step
        ).start()

    def vec_step(self, step):
        n = len(PIECES)
        own = self.v_half.at[self.feat] if step == 0 else self.v_sum.at[step - 1]
        self.remote(
            own, self.v_land.at[step], self.send_sem.at[n, step], self.recv_sem.at[n, step], step
        ).wait()
        self.v_sum[step] = own[...] + self.v_land[step]
        if step < 4:
            self.vec_go(step + 1)


    def tick(self, name, step=None):
        for action, at in self.table.get(name, ()):
            if at is None or isinstance(step, int):
                if at is None or at == step:
                    self.act(action)
            else:
                pl.when(step == at)(functools.partial(self.act, action))

    def act(self, action):
        verb, name = action
        if verb == SEND:
            self.go(name, 0)
        elif verb == FREE:
            for other in name:
                self.travel(other, 0).wait_send()
                self.gone.add((other, 0))
            for other in (S_MIX, S_KV) if name == REDUCES else (S_OUT, S_IN0, S_IN1, S_IN2):
                self.allow(other, FEAT)
        elif verb == BEGIN:
            for copy in self.copies_out(name):
                copy.start()
        elif verb == REUSE:
            near, far = self.copies_out(name)
            near.wait()
            far.wait_send()
        else:
            self.step(name, verb)

    def run(self):
        self.table, self.gone = {}, set()
        for name, at, actions in SCHEDULE:
            self.table.setdefault(name, []).extend((action, at) for action in actions)
        self.where_am_i()
        self.exchange()
        for copy in self.own:
            copy.start()
        self.start_weights()
        place = self.gs_half.at[self.feat]
        place[0:3, :] = self.gains[...]
        place[3:6, :] = self.shifts[...]
        self.greet()
        for copy in self.sent:
            copy.start()
        self.prepare()
        self.vec[...] = jnp.zeros(self.vec.shape, F32)
        self.landed(3)
        self.gs[...] = jnp.concatenate([self.gs_half[0], self.gs_half[1]], axis=1)
        self.landed(0)
        self.x[...] = self.x_t[...].T
        self.phases()
        self.act((BEGIN, INPUT_GRAD))
        self.v_half[0] = self.vec[:, : self.width // 2]
        self.v_half[1] = pltpu.roll(self.vec[...], self.width // 2, 1)[:, : self.width // 2]
        self.vec_go(0)
        for step in range(5):
            self.tick(END, step)
            self.vec_step(step)
        self.tick(END, 5)
        self.o_gain[...] = self.v_sum[4][0:3]
        self.o_shift[...] = self.v_sum[4][3:6]
        for name in PIECES:
            for step in range(5):
                if (name, step) not in self.gone:
                    self.travel(name, step).wait_send()
        for name in (LAYER_OUT, ENCODER_GRAD, INPUT_GRAD):
            if name != LAYER_OUT:
                self.act((REUSE, name))
            self.copies_out(name, local=False)[0].wait_recv()


def takes(step, *names):
    return tuple((step, name) for name in names)


SCHEDULE = (
    (FFN, 1, takes(SEND, EXPAND0)),
    (FFN, 3, takes(0, EXPAND0) + takes(SEND, EXPAND1)),
    (FFN, 5, takes(0, EXPAND1) + takes(SEND, EXPAND2)),
    (FFN_END, None, takes(SEND, REDUCE0, REDUCE1)),
    (NORM_3, None, takes(BEGIN, LAYER_OUT) + takes(0, EXPAND2, REDUCE0, REDUCE1)),
    (NORM_3, None, takes(FREE, REDUCES, EXPANDS)),
    (CROSS, 5, takes(1, EXPAND0, EXPAND1)),
    (CROSS, 7, takes(1, EXPAND2)),
    (MIXED, None, takes(SEND, S_MIX)),
    (KV, None, takes(SEND, S_KV) + takes(1, REDUCE0, REDUCE1)),
    (NORM_2, None, takes(0, S_MIX, S_KV) + takes(BEGIN, ENCODER_GRAD) + takes(REUSE, LAYER_OUT)),
    (SELF_START, None, takes(SEND, S_OUT) + takes(2, EXPAND0, EXPAND1)),
    (SELF, 1, takes(0, S_OUT) + takes(2, EXPAND2)),
    (SELF, 3, takes(2, REDUCE0, REDUCE1)),
    (SELF, 5, takes(3, EXPAND0, EXPAND1, EXPAND2)),
    (SELF, 7, takes(1, S_MIX, S_KV) + takes(3, REDUCE0, REDUCE1)),
    (IN, 0, takes(SEND, S_IN0) + takes(1, S_OUT)),
    (IN, 1, takes(SEND, S_IN1) + takes(0, S_IN0)),
    (IN, 2, takes(SEND, S_IN2) + takes(0, S_IN1) + takes(2, S_MIX, S_KV, S_OUT)),
    (NORM_1, 0, takes(0, S_IN2) + takes(4, EXPAND0, EXPAND1, EXPAND2)),
    (NORM_1, 1, takes(1, S_IN0, S_IN1, S_IN2) + takes(3, S_MIX, S_KV, S_OUT)),
    (END, 0, takes(4, REDUCE0, REDUCE1)),
    (END, 1, takes(2, S_IN0, S_IN1, S_IN2)),
    (END, 2, takes(4, S_MIX, S_KV, S_OUT)),
    (END, 3, takes(3, S_IN0, S_IN1, S_IN2)),
    (END, 5, takes(4, S_IN0, S_IN1, S_IN2)),
)


def spaces():
    return tuple(pl.BlockSpec(memory_space=s) for s in (pltpu.VMEM, pl.ANY, pltpu.SMEM))


def spill_outs(rows, hbm):
    return {
        f"spill{b}": (jax.ShapeDtypeStruct((HEADS, kn, qn), BF16), hbm)
        for b, (_, qn, _, kn) in enumerate(self_blocks(rows))
    }


COST = pl.CostEstimate(flops=50 * 10**9, bytes_accessed=40 * 10**6, transcendentals=0)


def local_layer(x, enc, og, t_len, s_len, gs, weights):
    rows, width = x.shape
    hidden = weights[5].shape[1]
    vmem, hbm, smem = spaces()
    shape = jax.ShapeDtypeStruct
    ins = dict(x=x, enc=enc, og=og, t_len=t_len, s_len=s_len, gs=gs)
    whole, pairs = shape((rows, width), F32), lambda n: (shape((2, width, n), BF16), hbm)
    outs = dict(
        layer_out=(whole, vmem),
        mid2=(whole, vmem),
        encoder_grad=(shape((rows, width), BF16), vmem),
        vec=(shape((8, width), F32), vmem),
        s_reduce=(shape((2, hidden // 2, width), BF16), vmem),
        s_expand=(shape((2, width, hidden // 2), BF16), vmem),
        to_kv=pairs(LANES[S_KV]),
        to_mix=pairs(LANES[S_MIX]),
        to_out=pairs(LANES[S_OUT]),
        to_in0=pairs(LANES[S_IN0]),
        to_in1=pairs(LANES[S_IN1]),
        to_in2=pairs(LANES[S_IN2]),
        **spill_outs(rows, hbm),
    )
    scratch = dict(scratch_of(rows, width, hidden), s_sem=pltpu.SemaphoreType.DMA((12,)))

    def kernel(*refs):
        first, rest = refs[: len(ins)], refs[len(ins) + 7 :]
        named = dict(zip(list(ins) + list(outs) + list(scratch), first + rest))
        LocalLayer(**share(sources=refs[len(ins) : len(ins) + 7], **named)).run()

    found = pl.pallas_call(
        kernel,
        out_shape=[o[0] for o in outs.values()],
        in_specs=[vmem, vmem, vmem, smem, smem, vmem] + [hbm] * 7,
        out_specs=[o[1] for o in outs.values()],
        scratch_shapes=list(scratch.values()),
        compiler_params=pltpu.CompilerParams(vmem_limit_bytes=VMEM_LIMIT),
        cost_estimate=COST,
    )(*ins.values(), *weights)
    return dict(zip(outs, found))


def whole_layer(inputs, encoder, output_grad, t_len, s_len, gains, shifts, weights):
    rows, half = inputs.shape[1] // 2, inputs.shape[0]
    width, hidden = 2 * half, weights[5].shape[1]
    shard = width // 16
    vmem, hbm, smem = spaces()
    shape = jax.ShapeDtypeStruct
    ins = dict(x_in=inputs, e_in=encoder, g_in=output_grad, t_len=t_len, s_len=s_len)
    ins.update(gains=gains, shifts=shifts)
    big, small = (shape(inputs.shape, F32), hbm), lambda *dims: (shape(dims, F32), vmem)
    outs = dict(
        layer_out=big,
        input_grad=big,
        encoder_grad=big,
        o_gain=small(3, half),
        o_shift=small(3, half),
        o_in=small(shard, 3 * half),
        o_out=small(shard, half),
        o_cq=small(shard, half),
        o_kv=small(shard, width),
        o_co=small(shard, half),
        o_expand=small(shard, hidden // 2),
        o_reduce=small(hidden // 16, half),
    )
    count = len(outs)
    outs.update(spill_outs(rows, hbm))
    vm, pieces = pltpu.VMEM, len(PIECES)
    dma, regular = pltpu.SemaphoreType.DMA, pltpu.SemaphoreType.REGULAR
    scratch = dict(
        scratch_of(rows, width, hidden),
        x=vm((rows, width), F32),
        gs=vm((8, width), F32),
        vec=vm((8, width), F32),
        mid2=vm((rows, width), F32),
        x_t=vm((width, rows), F32),
        grad_t=vm((width, rows), F32),
        e_t=vm((width, rows), BF16),
        gs_half=vm((2, 8, half), F32),
        s_reduce=vm((2, hidden // 2, width), BF16),
        s_expand=vm((2, width, hidden // 2), BF16),
        l_reduce=vm((hidden // 2, width), BF16),
        l_expand=vm((width, hidden // 2), BF16),
        v_half=vm((2, 8, half), F32),
        v_sum=vm((5, 8, half), F32),
        v_land=vm((5, 8, half), F32),
        in_own=dma((3,)),
        in_send=dma((4,)),
        in_recv=dma((4,)),
        out_own=dma((3,)),
        out_send=dma((3,)),
        out_recv=dma((3,)),
        send_sem=dma((pieces + 1, 5)),
        recv_sem=dma((pieces + 1, 5)),
        credit=regular((pieces, 4)),
    )
    ends = []
    for name in PIECES:
        dims = (shard, 2 * HIDDEN_TILE if name in EXPANDS else LANES.get(name))
        dims = (hidden // 32, half) if name in REDUCES else dims
        ends += [vm(dims, F32), vm(dims, BF16), vm(dims, BF16)]

    def kernel(*refs):
        first, rest = refs[: len(ins)], refs[len(ins) + 7 :]
        names = list(ins) + list(outs) + list(scratch)
        last = rest[len(outs) + len(scratch) :]
        named = dict(zip(names, first + rest))
        named.update(z_keep=last[0::3], z_send=last[1::3], z_land=last[2::3])
        RemoteLayer(**share(sources=refs[len(ins) : len(ins) + 7], **named)).run()

    found = pl.pallas_call(
        kernel,
        out_shape=[o[0] for o in outs.values()],
        in_specs=[hbm, hbm, hbm, smem, smem, vmem, vmem] + [hbm] * 7,
        out_specs=[o[1] for o in outs.values()],
        scratch_shapes=list(scratch.values()) + ends,
        compiler_params=pltpu.CompilerParams(
            vmem_limit_bytes=VMEM_LIMIT, collective_id=0, has_side_effects=True
        ),
        cost_estimate=COST,
    )(*ins.values(), *weights)
    return found[:count]


def hand_over(*arrays):
    count = len(arrays)

    def kernel(*refs):
        sources, targets, middle = (refs[n * count : (n + 1) * count] for n in range(3))
        before, after = refs[-2], refs[-1]
        comes = [pltpu.make_async_copy(sources[n], middle[n], before.at[n]) for n in range(count)]
        goes = [pltpu.make_async_copy(middle[n], targets[n], after.at[n]) for n in range(count)]
        for copy in comes:
            copy.start()
        for come, go in zip(comes, goes):
            come.wait()
            go.start()
        for copy in goes:
            copy.wait()

    _, hbm, _ = spaces()
    sems = [pltpu.SemaphoreType.DMA((count,))] * 2
    return pl.pallas_call(
        kernel,
        out_shape=[jax.ShapeDtypeStruct(a.shape, a.dtype) for a in arrays],
        in_specs=[hbm] * count,
        out_specs=[hbm] * count,
        scratch_shapes=[pltpu.VMEM(a.shape, a.dtype) for a in arrays] + sems,
        compiler_params=pltpu.CompilerParams(vmem_limit_bytes=VMEM_LIMIT),
    )(*arrays)


def gather_rows(part):
    return lax.all_to_all(part, "feat", split_axis=0, concat_axis=1, tiled=True)


def spread_rows(part):
    return lax.all_to_all(part, "feat", split_axis=1, concat_axis=0, tiled=True)


def over_feat(staged):
    return lax.psum_scatter(staged, "feat", scatter_dimension=0, tiled=True)[0]


def over_dp(part):
    return lax.psum_scatter(part, "dp", scatter_dimension=0, tiled=True).astype(F32)


def by_collectives(
    inputs, encoder, output_grad, target_lengths, source_lengths, gains, shifts, *weights
):
    width = weights[1].shape[0]
    half = width // 2
    vectors = jnp.concatenate([gains, shifts, jnp.zeros_like(gains[:2])], axis=0)
    vectors = lax.all_gather(vectors, "feat", axis=1, tiled=True)
    got = local_layer(
        gather_rows(inputs),
        gather_rows(encoder),
        gather_rows(output_grad),
        target_lengths,
        source_lengths,
        vectors,
        weights,
    )
    first = lax.axis_index("feat") == 0
    vec = lax.psum(got["vec"], ("dp", "feat"))
    vec = jnp.where(first, vec[:, :half], vec[:, half:])
    red = over_feat(got["s_reduce"])
    reduce_grad = over_dp(jnp.concatenate([red[:, :half], red[:, half:]], axis=0))
    expand_grad = over_dp(over_feat(got["s_expand"]))
    kv_grad = over_dp(over_feat(got["to_kv"]))
    mix = over_dp(over_feat(got["to_mix"]))
    out_grad = over_dp(over_feat(got["to_out"]))[:, :half]
    parts = [got["to_in0"], got["to_in1"], got["to_in2"]]
    wide = over_dp(over_feat(jnp.concatenate(parts, axis=2)))
    low, high = wide[:, : 3 * half], jnp.concatenate([wide[:, 896:960], wide[:, :896]], axis=1)
    return (
        spread_rows(got["layer_out"]),
        spread_rows(got["mid2"]),
        spread_rows(got["encoder_grad"]).astype(F32),
        vec[:3],
        vec[3:6],
        jnp.where(first, low, high),
        out_grad,
        mix[:, half:],
        kv_grad,
        mix[:, :half],
        expand_grad,
        reduce_grad,
    )


def by_remote_copies(
    inputs, encoder, output_grad, target_lengths, source_lengths, gains, shifts, *weights
):
    got = whole_layer(
        inputs.T, encoder.T, output_grad.T, target_lengths, source_lengths, gains, shifts, weights
    )
    got = hand_over(*got)
    return tuple(part.T for part in got[:3]) + tuple(got[3:])


def solution(mesh):
    rows, both = P("dp", "feat"), P(("dp", "feat"), None)
    columns, whole = P(None, "feat"), P()
    small = mesh.shape["dp"] == 16 and mesh.shape["feat"] == 2
    return jax.shard_map(
        by_remote_copies if small else by_collectives,
        mesh=mesh,
        in_specs=(rows, rows, rows, both, both, columns, columns) + (whole,) * 7,
        out_specs=(rows, rows, rows, columns, columns) + (rows,) * 7,
        check_vma=False,
    )
```

```python
import functools
import math

import jax
import jax.numpy as jnp
from jax import lax
from jax.experimental import pallas as pl
from jax.experimental.pallas import tpu as pltpu
from jax.sharding import PartitionSpec as P

HEADS = 8
LONGEST = 256
EPSILON = 1e-05
MASKED = -1e30
F32 = jnp.float32
BF16 = jnp.bfloat16
WINDOW = 256
HIDDEN_TILE = 512
EXPAND_LANES = 512
W_IN, W_OUT, W_CQ, W_KV, W_CO, W_EXPAND, W_REDUCE, W_IN_AGAIN = range(8)
FFN, FFN_END, NORM_3, CROSS_START, CROSS, MIXED, KV, NORM_2, SELF_START, SELF, IN, NORM_1, END = range(13)
EXPAND0, EXPAND1, EXPAND2, REDUCE0, REDUCE1, S_MIX, S_KV, S_OUT, S_IN0, S_IN1, S_IN2 = PIECES = range(11)
EXPANDS, REDUCES = (EXPAND0, EXPAND1, EXPAND2), (REDUCE0, REDUCE1)
INS, MIDDLE = (S_IN0, S_IN1, S_IN2), (S_MIX, S_KV)
FEAT, X, Y, Z1, Z2 = range(5)
QUERY_BLOCKS = ((0, 256), (256, 256), (512, 128))
VMEM_LIMIT = 65_000 * 2**10


def nn(left, right):
    return lax.dot_general(left, right, (((1,), (0,)), ((), ())), preferred_element_type=F32)


def nt(left, right):
    return lax.dot_general(left, right, (((1,), (1,)), ((), ())), preferred_element_type=F32)


def self_blocks(rows):
    found = []
    for start, size in QUERY_BLOCKS:
        first = max(0, start - LONGEST)
        found.append((start, size, first, start + size - first))
    return found


def cross_blocks(rows):
    return [(start, size, 0, min(rows, start + size + LONGEST)) for start, size in QUERY_BLOCKS]


def gelu_parts(value):
    root = math.sqrt(2.0 / math.pi)
    square = value * value
    inner = value * (root + (root * 0.044715) * square)
    bent = jnp.tanh(inner)
    up = 0.5 + 0.5 * bent
    slope = (0.5 * value) * (1.0 - bent * bent) * (root + (3.0 * root * 0.044715) * square)
    return value * up, up + slope


def norm_stats(value):
    mean = jnp.mean(value, axis=1, keepdims=True)
    second = jnp.mean(value * value, axis=1, keepdims=True)
    scale = lax.rsqrt(second - mean * mean + EPSILON)
    return (value - mean) * scale, scale


def pack_halves(left, right):
    width = left.shape[1]
    low = lax.broadcasted_iota(jnp.int32, left.shape, 1) < width // 2
    return (
        jnp.where(low, left, pltpu.roll(right, width // 2, 1)),
        jnp.where(low, pltpu.roll(left, width // 2, 1), right),
    )


def in_spans(width):
    half, part = 3 * width // 2, 384
    high = half + 64
    yield S_IN0, ((0, part), (high, part))
    yield S_IN1, ((part, part), (high + part, part))
    yield S_IN2, ((2 * part, 256), (high + 2 * part, 128))


class Layer:
    def __init__(self, **refs):
        self.__dict__.update(refs)
        self.rows, self.width = self.branch1.shape
        self.hidden = self.w_expand.shape[1]
        self.head = self.width // HEADS
        most = -(-self.rows // 256) * 128
        self.halves = [(0, most), (most, self.rows - most)]


    def segments(self, lengths, shape, axis):
        place = lax.broadcasted_iota(jnp.int32, shape, axis)
        found = jnp.zeros(shape, jnp.int32)
        end = jnp.int32(0)
        for slot in range(lengths.shape[1]):
            end = end + lengths[0, slot]
            found = found + jnp.where(place >= end, 1, 0)
        return found, place < end, place

    def prepare(self):
        rows = self.rows
        lane = lax.broadcasted_iota(jnp.int32, (rows, 128), 1)
        columns = []
        for lengths in (self.t_len, self.s_len):
            seg, valid, _ = self.segments(lengths, (rows, 128), 0)
            columns.append(jnp.where(valid, seg, -2))
        self.t_col[...] = jnp.where(lane < 64, *columns)
        seg, valid, _ = self.segments(self.t_len, (8, rows), 1)
        self.t_row[...] = jnp.where(valid, seg, -1)

    def kept(self, part):
        return jnp.where(self.t_col[part, 0:1] >= 0, 1.0, 0.0).astype(F32)

    def make_bias(self, blocks, lane, causal):
        for ref, (q0, qn, k0, kn) in zip(self.bias, blocks):
            allowed = self.t_col[k0 : k0 + kn, lane : lane + 1] == self.t_row[0:1, q0 : q0 + qn]
            if causal:
                key = lax.broadcasted_iota(jnp.int32, (kn, qn), 0) + k0
                query = lax.broadcasted_iota(jnp.int32, (kn, qn), 1) + q0
                allowed = allowed & (key <= query)
            ref[0:kn, :] = jnp.where(allowed, 0.0, MASKED).astype(F32)


    def window(self, head):
        tiles = jnp.minimum((head * self.head) // 128, (self.width - WINDOW) // 128)
        start = pl.multiple_of(tiles * 128, 128)
        lane = lax.broadcasted_iota(jnp.int32, (8, WINDOW), 1) + start
        mine = (lane >= head * self.head) & (lane < (head + 1) * self.head)
        return start, jnp.where(mine, 1.0, 0.0).astype(F32)[0:1]

    def attend(self, queries, q_at, keys, k_at, mixed_t, blocks):
        factor = math.log2(math.e) / math.sqrt(self.head)

        @pl.loop(0, HEADS, unroll=2)
        def _(head):
            start, mine = self.window(head)
            band = pl.ds(pl.multiple_of(head * self.head, 16), self.head)
            for b, (q0, qn, k0, kn) in enumerate(blocks):
                query = queries[q0 : q0 + qn, pl.ds(q_at + start, WINDOW)]
                query = (query.astype(F32) * mine).astype(BF16)
                key = keys[k0 : k0 + kn, pl.ds(k_at + start, WINDOW)]
                scores = nt(key, query) + self.bias[b][0:kn, :]
                largest = jnp.max(scores, axis=0, keepdims=True)
                expo = jnp.exp2((scores - largest) * factor)
                total = jnp.sum(expo, axis=0, keepdims=True)
                weights = (expo * (1.0 / total)).astype(BF16)
                self.p[b][head, 0:kn, :] = weights
                mixed = nn(self.v_t[band, k0 : k0 + kn], weights)
                mixed_t[band, q0 : q0 + qn] = mixed.astype(BF16)

    def attend_back(self, queries, q_at, keys, k_at, values, v_at, mixed_t, blocks, name):
        scale = 1.0 / math.sqrt(self.head)
        self.dk[...] = jnp.zeros(self.dk.shape, F32)
        self.dv[...] = jnp.zeros(self.dv.shape, F32)

        @pl.loop(0, HEADS // 2)
        def _(pair):
            for head in (2 * pair, 2 * pair + 1):
                start, mine = self.window(head)
                band = pl.ds(pl.multiple_of(head * self.head, 16), self.head)
                lanes = pl.ds(start, WINDOW)
                for b, (q0, qn, k0, kn) in enumerate(blocks):
                    query = queries[q0 : q0 + qn, pl.ds(q_at + start, WINDOW)]
                    query = (query.astype(F32) * mine).astype(BF16)
                    grad = (self.g[q0 : q0 + qn, lanes].astype(F32) * mine).astype(BF16)
                    value = values[k0 : k0 + kn, pl.ds(v_at + start, WINDOW)]
                    weights = self.p[b][head, 0:kn, :]
                    product = self.g_t[band, q0 : q0 + qn].astype(F32) * mixed_t[band, q0 : q0 + qn].astype(F32)
                    centre = jnp.sum(product, axis=0, keepdims=True)
                    grad_w = nt(value, grad)
                    grad_s = (weights.astype(F32) * (grad_w - centre)).astype(BF16)
                    self.dv[k0 : k0 + kn, lanes] += nn(weights, grad)
                    self.dk[k0 : k0 + kn, lanes] += nn(grad_s, query)
                    grad_q = nn(self.k_t[band, k0 : k0 + kn], grad_s)
                    self.dq_t[band, q0 : q0 + qn] = (grad_q * scale).astype(BF16)
            self.tick(name, pair)


    def norm_to(self, value, which, start, size, target):
        normed, _ = norm_stats(value)
        gain, shift = self.gs[which : which + 1, :], self.gs[3 + which : 4 + which, :]
        target[start : start + size, :] = (normed * gain + shift).astype(BF16)

    def norm_back(self, grad, value, which, first):
        normed, scale = norm_stats(value)
        scaled = grad * self.gs[which : which + 1, :]
        one = jnp.mean(scaled, axis=1, keepdims=True)
        two = jnp.mean(scaled * normed, axis=1, keepdims=True)
        gain = jnp.sum(grad * normed, axis=0, keepdims=True)
        shift = jnp.sum(grad, axis=0, keepdims=True)
        if first:
            self.vec[which : which + 1, :] = gain
            self.vec[3 + which : 4 + which, :] = shift
        else:
            self.vec[which : which + 1, :] += gain
            self.vec[3 + which : 4 + which, :] += shift
        return (scaled - one - normed * two) * scale


    def forward_self(self):
        width = self.width
        for start, size in self.halves:
            part = slice(start, start + size)
            self.norm_to(self.x[part, :], 0, start, size, self.g)
        self.arrive(W_IN)
        for col in range(0, 3 * width, width):
            self.proj[:, col : col + width] = nn(
                self.g[...], self.w_in[:, col : col + width]
            ).astype(BF16)
        self.v_t[...] = self.proj[:, 2 * width :].T
        self.make_bias(self_blocks(self.rows), 0, True)
        self.attend(self.proj, 0, self.proj, width, self.mixed1_t, self_blocks(self.rows))

    def forward_cross(self):
        width = self.width
        self.spill_weights()
        self.arrive(W_KV)
        enc = self.encoder_rows(self.k_t)
        for col in range(0, 2 * width, width):
            self.memory[:, col : col + width] = nn(
                enc[...], self.w_kv[:, col : col + width]
            ).astype(BF16)
        self.v_t[...] = self.memory[:, width:].T
        self.g[...] = self.mixed1_t[...].T
        self.arrive(W_OUT)
        self.arrive(W_CQ)
        for start, size in self.halves:
            part = slice(start, start + size)
            branch = (nn(self.g[part, :], self.w_out[...]) * self.kept(part)).astype(BF16)
            mid = self.x[part, :] + branch.astype(F32)
            self.branch1[part, :] = branch
            self.norm_to(mid, 1, start, size, self.normed2)
            self.cq[part, :] = nn(self.normed2[part, :], self.w_cq[...]).astype(BF16)
        self.make_bias(cross_blocks(self.rows), 64, False)
        self.spill_wait()
        self.attend(self.cq, 0, self.memory, 0, self.mixed2_t, cross_blocks(self.rows))

    def mid1_rows(self, part):
        return self.x[part, :] + self.branch1[part, :].astype(F32)

    def feed_forward(self):
        width, tile = self.width, HIDDEN_TILE
        self.g[...] = self.mixed2_t[...].T
        self.arrive(W_CO)
        for start, size in self.halves:
            part = slice(start, start + size)
            branch = (nn(self.g[part, :], self.w_co[...]) * self.kept(part)).astype(BF16)
            mid = self.mid1_rows(part) + branch.astype(F32)
            self.mid2[part, :] = mid
            self.norm_to(mid, 2, start, size, self.normed3)
        self.k_t[...] = self.normed3[...].T
        self.landed(2)
        for start, size in self.halves:
            part = slice(start, start + size)
            self.g[part, :] = (self.grad_rows(part) * self.kept(part)).astype(BF16)
        self.dk[...] = jnp.zeros(self.dk.shape, F32)
        self.dv[...] = jnp.zeros(self.dv.shape, F32)
        self.arrive(W_EXPAND)
        self.arrive(W_REDUCE)

        @pl.loop(0, self.hidden // (2 * tile))
        def _(step):
            actives = []
            low = pl.multiple_of(step * tile, tile)
            for side in range(2):
                at = pl.multiple_of(side * (self.hidden // 2) + step * tile, tile)
                expand = self.w_expand[:, pl.ds(at, tile)]
                reduce = self.w_reduce[pl.ds(at, tile), :]
                value = nn(self.normed3[...], expand).astype(BF16).astype(F32)
                active, slope = gelu_parts(value)
                active = active.astype(BF16)
                grad = (nt(self.g[...], reduce) * slope).astype(BF16)
                self.dk[...] += nn(active, reduce)
                self.dv[...] += nt(grad, expand)
                self.put_expand(step, side, low, nn(self.k_t[...], grad))
                actives.append(active)
            for part in range(0, tile, 256):
                sides = [nn(active[:, part : part + 256].T, self.g[...]) for active in actives]
                for side, packed in enumerate(pack_halves(*sides)):
                    self.put_reduce(step * (tile // 256) + part // 256, side, low + part, packed)
            self.tick(FFN, step)

        self.tick(FFN_END)
        for n, (start, size) in enumerate(self.halves):
            part = slice(start, start + size)
            mid = self.mid2[part, :]
            branch = (self.dk[part, :] * self.kept(part)).astype(BF16)
            self.put_layer_out(part, mid + branch.astype(F32))
            grad = self.dv[part, :].astype(BF16).astype(F32)
            self.mid2[part, :] = self.grad_rows(part) + self.norm_back(grad, mid, 2, n == 0)
            self.tick(NORM_3, n)

    def backward_cross(self):
        width = self.width
        self.mid_grad[...] = (self.mid2[...] * self.kept(slice(None))).astype(BF16)
        self.g[...] = nt(self.mid_grad[...], self.w_co[...]).astype(BF16)
        self.g_t[...] = self.g[...].T
        self.k_t[...] = self.memory[:, 0:width].T
        self.tick(CROSS_START)
        self.attend_back(
            self.cq, 0, self.memory, 0, self.memory, width, self.mixed2_t, cross_blocks(self.rows), CROSS
        )
        self.refetch()
        out_grad = nn(self.mixed2_t[...], self.mid_grad[...])
        self.fetch_weights()
        scale = 1.0 / math.sqrt(self.head)
        self.gmem[:, 0:width] = (self.dk[...] * scale).astype(BF16)
        self.gmem[:, width : 2 * width] = self.dv[...].astype(BF16)
        self.g[...] = self.dq_t[...].T
        self.k_t[...] = self.normed2[...].T
        for side, packed in enumerate(pack_halves(out_grad, nn(self.k_t[...], self.g[...]))):
            self.put_rows(S_MIX, side, packed)
        self.tick(MIXED)
        enc_t = self.encoder_columns(self.k_t)
        for side in range(2):
            self.put_rows(
                S_KV, side, nn(enc_t[...], self.gmem[:, side * width : (side + 1) * width])
            )
        self.tick(KV)
        for n, (start, size) in enumerate(self.halves):
            part = slice(start, start + size)
            self.put_encoder_grad(part, nt(self.gmem[part, 0 : 2 * width], self.w_kv[...]).astype(BF16))
            grad = nt(self.g[part, :], self.w_cq[...]).astype(BF16).astype(F32)
            self.mid2[part, :] += self.norm_back(grad, self.mid1_rows(part), 1, n == 0)
            self.tick(NORM_2, n)

    def backward_self(self):
        width = self.width
        self.mid_grad[...] = (self.mid2[...] * self.kept(slice(None))).astype(BF16)
        self.g[...] = nt(self.mid_grad[...], self.w_out[...]).astype(BF16)
        self.g_t[...] = self.g[...].T
        self.k_t[...] = self.proj[:, width : 2 * width].T
        self.put_rows_split(S_OUT, nn(self.mixed1_t[...], self.mid_grad[...]))
        self.fetch_wait()
        self.tick(SELF_START)
        self.attend_back(
            self.proj, 0, self.proj, width, self.proj, 2 * width, self.mixed1_t, self_blocks(self.rows), SELF
        )
        scale = 1.0 / math.sqrt(self.head)
        self.gmem[:, 0:width] = self.dq_t[...].T
        self.gmem[:, width : 2 * width] = (self.dk[...] * scale).astype(BF16)
        self.gmem[:, 2 * width :] = self.dv[...].astype(BF16)
        for start, size in self.halves:
            self.norm_to(self.x[start : start + size, :], 0, start, size, self.g)
        self.k_t[...] = self.g[...].T
        for n, (name, spans) in enumerate(in_spans(width)):
            for side, (col, size) in enumerate(spans):
                value = nn(self.k_t[...], self.gmem[:, col : col + size])
                if n == 2 and side == 1:
                    odd = nn(self.k_t[...], self.gmem[:, 896:1024])
                    value = jnp.concatenate([value, pltpu.roll(odd, 64, 1)], axis=1)
                self.put_rows(name, side, value)
            self.tick(IN, n)
        self.arrive(W_IN_AGAIN)
        for n, (start, size) in enumerate(self.halves):
            part = slice(start, start + size)
            grad = nt(self.gmem[part, :], self.w_in[...]).astype(BF16).astype(F32)
            self.put_input_grad(
                part, self.mid2[part, :] + self.norm_back(grad, self.x[part, :], 0, n == 0)
            )
            self.tick(NORM_1, n)


def scratch_of(rows, width, hidden):
    wide = [k[3] for k in cross_blocks(rows)]
    vm = pltpu.VMEM
    named = dict(
        w_in=vm((width, 3 * width), BF16),
        w_out=vm((width, width), BF16),
        w_cq=vm((width, width), BF16),
        w_kv=vm((width, 2 * width), BF16),
        w_co=vm((width, width), BF16),
        w_expand=vm((width, hidden), BF16),
        w_reduce=vm((hidden, width), BF16),
        t_col=vm((rows, 128), jnp.int32),
        t_row=vm((8, rows), jnp.int32),
        proj=vm((rows, 3 * width), BF16),
        v_t=vm((width, rows), BF16),
        mixed1_t=vm((width, rows), BF16),
        branch1=vm((rows, width), BF16),
        pair=vm((2, rows, width), BF16),
        normed3=vm((rows, width), BF16),
        g=vm((rows, width), BF16),
        k_t=vm((width, rows), BF16),
        dk=vm((rows, width), F32),
        dv=vm((rows, width), F32),
        w_sem=pltpu.SemaphoreType.DMA((7,)),
        p_sem=pltpu.SemaphoreType.DMA((3,)),
        again_sem=pltpu.SemaphoreType.DMA(()),
    )
    for b, (_, qn, _, kn) in enumerate(cross_blocks(rows)):
        named[f"p{b}"] = vm((HEADS, kn, qn), BF16)
    return named


class SavedLayer(Layer):
    def put_rows_split(self, name, value):
        turned = pltpu.roll(value, value.shape[1] // 2, 1)
        for side, part in enumerate((value, turned)):
            self.put_rows(name, side, part[:, : LANES[name]])

    def start_weights(self):
        targets = (self.w_in, self.w_out, self.w_cq, self.w_kv, self.w_co, self.w_expand, self.w_reduce)
        self.copies = {
            n: pltpu.make_async_copy(self.sources[n], target, self.w_sem.at[n])
            for n, target in enumerate(targets)
        }
        for copy in self.copies.values():
            copy.start()

    def refetch(self):
        self.copies[W_IN_AGAIN] = pltpu.make_async_copy(
            self.sources[W_IN], self.w_in, self.again_sem
        )
        self.copies[W_IN_AGAIN].start()

    def arrive(self, name):
        self.copies[name].wait()

    def spill_copies(self, back):
        found = []
        for b, (_, _, _, kn) in enumerate(self_blocks(self.rows)):
            here, there = self.p[b].at[:, 0:kn, :], self.spill[b]
            pair = (there, here) if back else (here, there)
            found.append(pltpu.make_async_copy(*pair, self.p_sem.at[b]))
        return found

    def spill_weights(self):
        for copy in self.spill_copies(False):
            copy.start()

    def spill_wait(self):
        for copy in self.spill_copies(False):
            copy.wait()

    def fetch_weights(self):
        for copy in self.spill_copies(True):
            copy.start()

    def fetch_wait(self):
        for copy in self.spill_copies(True):
            copy.wait()

    def phases(self):
        self.forward_self()
        self.forward_cross()
        self.feed_forward()
        self.backward_cross()
        self.backward_self()


def share(p0, p1, p2, spill0, spill1, spill2, sources, pair, **named):
    rows, width = named["branch1"].shape
    first, expand, reduce, proj = (named[n] for n in ("w_in", "w_expand", "w_reduce", "proj"))

    def place(name, side):
        if name in (S_KV, S_MIX):
            at = side * width + (2 * width if name == S_MIX else 0)
            return reduce, pl.multiple_of(at, width), 0
        if name == S_OUT:
            return pair.at[side], 0, 0
        if name == S_IN2:
            return expand, 0, pl.multiple_of(4 * width + side * 256, 128)
        at = side * 768 + (384 if name == S_IN1 else 0)
        return proj, 0, pl.multiple_of(at, 128)

    return dict(
        named,
        g_t=named["v_t"],
        dq_t=named["normed3"],
        memory=first.at[:, 0 : 2 * width],
        cq=first.at[:, 2 * width : 3 * width],
        gmem=expand.at[:, 0 : 3 * width],
        mid_grad=expand.at[:, 3 * width : 4 * width],
        bias=[named["dk"].at[0:kn, q0 : q0 + qn] for q0, qn, _, kn in cross_blocks(rows)],
        p=(p0, p1, p2),
        spill=(spill0, spill1, spill2),
        sources=sources,
        normed2=pair.at[0],
        mixed2_t=pair.at[1],
        place=place,
    )


LANES = {S_MIX: 640, S_KV: 640, S_OUT: 384, S_IN0: 384, S_IN1: 384, S_IN2: 256}


class LocalLayer(SavedLayer):
    def staged(self, names):
        targets = {S_KV: self.to_kv, S_MIX: self.to_mix, S_OUT: self.to_out}
        targets.update({S_IN0: self.to_in0, S_IN1: self.to_in1, S_IN2: self.to_in2})
        found = []
        for name in names:
            for side in range(2):
                base, row, col = self.place(name, side)
                found.append(
                    pltpu.make_async_copy(
                        base.at[pl.ds(row, self.width), pl.ds(col, LANES[name])],
                        targets[name].at[side],
                        self.s_sem.at[2 * (name - S_MIX) + side],
                    )
                )
        return found

    def tick(self, name, step=None):
        for when, pieces in ((KV, (S_MIX, S_KV)), (SELF_START, (S_OUT,)), (NORM_1, (S_IN0, S_IN1, S_IN2))):
            if name == when and step in (None, 0):
                for copy in self.staged(pieces):
                    copy.start()

    def encoder_columns(self, spare):
        spare[...] = self.enc[...].T
        return spare

    def encoder_rows(self, spare):
        return self.enc

    def landed(self, n):
        pass

    def grad_rows(self, part):
        return self.og[part, :]

    def put_rows(self, name, side, value):
        base, row, col = self.place(name, side)
        base[pl.ds(row, self.width), pl.ds(col, value.shape[1])] = value.astype(BF16)

    def put_expand(self, step, side, low, value):
        self.s_expand[side, :, pl.ds(low, value.shape[1])] = value.astype(BF16)

    def put_reduce(self, step, side, low, value):
        self.s_reduce[side, pl.ds(low, value.shape[0]), :] = value.astype(BF16)

    def put_layer_out(self, part, value):
        self.layer_out[part, :] = value

    def put_input_grad(self, part, value):
        self.mid2[part, :] = value

    def put_encoder_grad(self, part, value):
        self.encoder_grad[part, :] = value

    def run(self):
        self.start_weights()
        self.prepare()
        self.vec[...] = jnp.zeros(self.vec.shape, F32)
        self.phases()
        for copy in self.staged((S_MIX, S_KV, S_OUT, S_IN0, S_IN1, S_IN2)):
            copy.wait()


MESH = pl.DeviceIdType.MESH
LAYER_OUT, ENCODER_GRAD, INPUT_GRAD = range(3)
SEND, FREE, BEGIN, REUSE, GO = range(5, 10)
ORDER = {
    EXPAND0: (Z1, X, Y),
    EXPAND1: (Z1, Y, X),
    EXPAND2: (Z1, X, Y),
    REDUCE0: (Y, X, Z1),
    REDUCE1: (X, Y, Z1),
    S_MIX: (Z1, Y, X),
    S_KV: (X, Y, Z1),
    S_OUT: (Z1, Y, X),
    S_IN0: (X, Y, Z1),
    S_IN1: (Y, X, Z1),
    S_IN2: (Z1, X, Y),
}


class RemoteLayer(SavedLayer):
    def where_am_i(self):
        self.dp, self.feat = lax.axis_index("dp"), lax.axis_index("feat")
        bits = [lax.rem(lax.div(self.dp, 1 << n), 2) for n in range(4)]
        self.bit = dict(zip((X, Y, Z1, Z2), bits))
        self.peer = {FEAT: (self.dp, 1 - self.feat)}
        for n, link in enumerate((X, Y, Z1, Z2)):
            self.peer[link] = (self.dp + (1 << n) * (1 - 2 * bits[n]), self.feat)

    def remote(self, source, target, send, receive, link):
        return pltpu.make_async_remote_copy(
            source, target, send, receive, device_id=self.peer[link], device_id_type=MESH
        )

    def greet(self):
        barrier = pltpu.get_barrier_semaphore()
        for link in range(5):
            pl.semaphore_signal(barrier, 1, device_id=self.peer[link], device_id_type=MESH)
        pl.semaphore_wait(barrier, 5)


    def mine(self, size):
        return pl.ds(pl.multiple_of(self.feat * size, size), size)

    def other(self, size):
        return pl.ds(pl.multiple_of((1 - self.feat) * size, size), size)

    def exchange(self):
        rows, half = self.rows, self.width // 2
        pairs = ((self.x_in, self.x_t), (self.e_in, self.e_t), (self.g_in, self.grad_t))
        self.own, self.sent = [], []
        for n, (source, target) in enumerate(pairs):
            place = target.at[self.mine(half), :]
            mine, other = source.at[:, self.mine(rows)], source.at[:, self.other(rows)]
            self.own.append(pltpu.make_async_copy(mine, place, self.in_own.at[n]))
            self.sent.append(self.remote(other, place, self.in_send.at[n], self.in_recv.at[n], FEAT))
        place = self.gs_half.at[self.feat]
        self.sent.append(self.remote(place, place, self.in_send.at[3], self.in_recv.at[3], FEAT))

    def landed(self, n):
        if n < 3:
            self.own[n].wait()
        self.sent[n].wait()

    def encoder_rows(self, spare):
        self.landed(1)
        spare[...] = self.e_t[...].T
        return spare

    def encoder_columns(self, spare):
        return self.e_t

    def grad_rows(self, part):
        return self.grad_t[:, part].T


    def copies_out(self, name, local=True):
        source = self.grad_t if name == ENCODER_GRAD else self.x_t
        half = self.width // 2
        place = (self.layer_out, self.encoder_grad, self.input_grad)[name].at[:, self.mine(self.rows)]
        far = self.remote(
            source.at[self.other(half), :], place, self.out_send.at[name], self.out_recv.at[name], FEAT
        )
        if not local:
            return (far,)
        near = pltpu.make_async_copy(source.at[self.mine(half), :], place, self.out_own.at[name])
        return near, far

    def put_layer_out(self, part, value):
        self.x_t[:, part] = value.T

    def put_encoder_grad(self, part, value):
        self.grad_t[:, part] = value.astype(F32).T

    def put_input_grad(self, part, value):
        self.x_t[:, part] = value.T


    def spot(self, name, side, row, count):
        if name in EXPANDS:
            lanes = pl.ds(EXPAND_LANES * (name - EXPAND0), EXPAND_LANES)
            return self.s_expand.at[side, pl.ds(row, count), lanes]
        if name in REDUCES:
            height = self.s_reduce.shape[1] // 2
            return self.s_reduce.at[side, pl.ds((name - REDUCE0) * height + row, count), :]
        base, top, left = self.place(name, side)
        return base.at[pl.ds(top + row, count), pl.ds(left, LANES[name])]

    def landing(self, name, side, row, count):
        if name in EXPANDS:
            lanes = pl.ds(EXPAND_LANES * (name - EXPAND0), EXPAND_LANES)
            return self.l_expand.at[pl.ds(row, count), lanes]
        if name in REDUCES:
            height = self.s_reduce.shape[1] // 2
            return self.l_reduce.at[pl.ds((name - REDUCE0) * height + row, count), :]
        if name in (S_KV, S_MIX):
            first = self.width if name == S_MIX else 0
            return self.s_reduce.at[side, pl.ds(first + row, count), :]
        return self.s_expand.at[side, pl.ds(row, count), pl.ds(384 * (name - S_OUT), LANES[name])]

    def landing_one(self, name, row, count):
        half = self.width // 2
        first = {S_IN0: 0, S_IN1: half, S_IN2: 2 * self.width}[name]
        at = pl.multiple_of((1 - self.feat) * self.width, self.width) + first + row
        return self.w_reduce.at[pl.ds(at, count), pl.ds(0, LANES[name])]

    def plan(self, name):
        quarter = (self.s_reduce.shape[1] // 2 if name in REDUCES else self.width) // 4
        links = ORDER[name]
        one = self.bit[links[0]] * 2 * quarter
        two = one + self.bit[links[1]] * quarter
        three = two + self.bit[links[2]] * (quarter // 2)
        return quarter, links, (one, two, three)

    def travel(self, name, step):
        n = name
        quarter, links, (one, two, _) = self.plan(name)
        here, there = self.feat, 1 - self.feat
        if step == 0:
            link, count = FEAT, 4 * quarter
            source = self.spot(name, there, 0, count)
            target = self.landing(name, here, 0, count)
        elif step == 1:
            link, count = links[0], 2 * quarter
            source = self.spot(name, here, (1 - self.bit[link]) * count, count)
            target = self.landing(name, there, 0, count)
            if name in INS:
                target = self.landing_one(name, 0, count)
        elif step == 2:
            link, count = links[1], quarter
            source = self.spot(name, here, one + (1 - self.bit[link]) * count, count)
            target = self.landing(name, there, 2 * quarter, count)
        elif step == 3:
            link, count = links[2], quarter // 2
            source = self.spot(name, here, two + (1 - self.bit[link]) * count, count)
            target = self.landing(name, there, 3 * quarter, count)
        else:
            link, source, target = Z2, self.z_send[n], self.z_land[n]
        return self.remote(source, target, self.send_sem.at[n, step], self.recv_sem.at[n, step], link)

    def credit_at(self, name, link):
        return self.credit.at[name, link]

    def allow(self, name, link):
        pl.semaphore_signal(self.credit_at(name, link), 1, device_id=self.peer[link], device_id_type=MESH)

    def go(self, name, step):
        link = (FEAT, *ORDER[name], Z2)[step]
        if step in (1, 2, 3) or (step == 0 and name >= S_MIX):
            pl.semaphore_wait(self.credit_at(name, link), 1)
        self.travel(name, step).start()

    def add(self, name, row, count, from_row, step):
        mine = self.spot(name, self.feat, row, count)
        if step == 1 and name in INS:
            came = self.landing_one(name, from_row, count)
        else:
            came = self.landing(name, 1 - self.feat, from_row, count)
        mine[...] = mine[...] + came[...]

    def step(self, name, step):
        n = name
        quarter, links, (one, two, three) = self.plan(name)
        self.travel(name, step).wait_recv()
        if step == 0:
            for n in range(4):
                self.add(name, n * quarter, quarter, n * quarter, step)
            for link in links[1:] if name in INS else links:
                self.allow(name, link)
        elif step == 1:
            out, kept = (1 - self.bit[links[1]]) * quarter, self.bit[links[1]] * quarter
            self.add(name, one + out, quarter, out, step)
            self.go(name, 2)
            self.add(name, one + kept, quarter, kept, step)
        elif step == 2:
            half = quarter // 2
            out, kept = (1 - self.bit[links[2]]) * half, self.bit[links[2]] * half
            self.add(name, two + out, half, 2 * quarter + out, step)
            self.go(name, 3)
            self.add(name, two + kept, half, 2 * quarter + kept, step)
        elif step == 3:
            half = quarter // 2
            value = self.spot(name, self.feat, three, half)[...].astype(F32)
            value = value + self.landing(name, 1 - self.feat, 3 * quarter, half)[...].astype(F32)
            if name in REDUCES:
                wide = self.width // 2
                low, high = value[:, :wide], pltpu.roll(value, wide, 1)[:, :wide]
            else:
                low, high = value[: half // 2], value[half // 2 :]
            first = self.bit[Z2] == 0
            self.z_keep[n][...] = jnp.where(first, low, high)
            self.z_send[n][...] = jnp.where(first, high, low).astype(BF16)
            self.go(name, 4)
        else:
            value = self.z_keep[n][...] + self.z_land[n][...].astype(F32)
            self.finish(name, value)

    def finish(self, name, value):
        half = self.width // 2
        if name in EXPANDS:
            at = EXPAND_LANES * (name - EXPAND0)
            self.o_expand[:, at : at + value.shape[1]] = value
        elif name in REDUCES:
            at = value.shape[0] * (name - REDUCE0)
            self.o_reduce[at : at + value.shape[0], :] = value
        elif name == S_KV:
            self.o_kv[...] = value
        elif name == S_MIX:
            self.o_co[...] = value[:, :half]
            self.o_cq[...] = pltpu.roll(value, half, 1)[:, :half]
        elif name == S_OUT:
            self.o_out[...] = value[:, :half]
        elif name != S_IN2:
            self.z_keep[name][...] = value
        else:
            parts = [self.z_keep[S_IN0][...], self.z_keep[S_IN1][...], value]
            wide = jnp.concatenate(parts, axis=1)
            lane = lax.broadcasted_iota(jnp.int32, wide.shape, 1)
            moved = pltpu.roll(wide, 64, 1)
            moved = jnp.where(lane < 64, pltpu.roll(wide, 1024 - 896, 1), moved)
            self.o_in[...] = jnp.where(self.feat == 0, wide, moved)[:, : 3 * half]

    def seat(self, name, block):
        bits = {Z1: block // 4, Y: block // 2 % 2, X: block % 2}
        a, b, c = (bits[link] for link in ORDER[name])
        return 4 * a + 2 * b + c

    def in_pairs(self, value):
        rows = value.shape[0] // 16
        for n in range(8):
            part = [value[at * rows : (at + 1) * rows] for at in (n, n + 8)]
            yield n, jnp.concatenate(part, axis=0).astype(BF16)

    def put_rows(self, name, side, value):
        base, top, left = self.place(name, side)
        for block, part in self.in_pairs(value):
            row, count = self.seat(name, block) * part.shape[0], part.shape[0]
            base[pl.ds(top + row, count), pl.ds(left, part.shape[1])] = part

    def put_expand(self, step, side, low, value):
        which = lax.div(step * value.shape[1], EXPAND_LANES)
        for block, part in self.in_pairs(value):
            seats = [self.seat(name, block) for name in EXPANDS]
            seat = jnp.where(which == 0, seats[0], jnp.where(which == 1, seats[1], seats[2]))
            at = pl.multiple_of(seat * part.shape[0], 16)
            self.s_expand[side, pl.ds(at, part.shape[0]), pl.ds(low, value.shape[1])] = part

    def put_reduce(self, step, side, low, value):
        count, piece = 32, self.s_reduce.shape[1] // 2
        eighth = piece // 8
        for n in range(value.shape[0] // count):
            row = step * value.shape[0] + n * count
            block, rest = lax.div(row, 2 * eighth), lax.rem(row, 2 * eighth)
            bits = {Z1: lax.div(block, 4), Y: lax.rem(lax.div(block, 2), 2), X: lax.rem(block, 2)}
            which, inside = lax.div(rest, eighth), lax.rem(rest, eighth)
            seats = []
            for name in REDUCES:
                a, b, c = (bits[link] for link in ORDER[name])
                seats.append(4 * a + 2 * b + c)
            at = which * piece + jnp.where(which == 0, *seats) * eighth + inside
            part = value[n * count : (n + 1) * count].astype(BF16)
            self.s_reduce[side, pl.ds(pl.multiple_of(at, 32), count), :] = part


    def vec_go(self, step):
        n = len(PIECES)
        source = self.v_half.at[1 - self.feat] if step == 0 else self.v_sum.at[step - 1]
        self.remote(
            source, self.v_land.at[step], self.send_sem.at[n, step], self.recv_sem.at[n, step], step
        ).start()

    def vec_step(self, step):
        n = len(PIECES)
        own = self.v_half.at[self.feat] if step == 0 else self.v_sum.at[step - 1]
        self.remote(
            own, self.v_land.at[step], self.send_sem.at[n, step], self.recv_sem.at[n, step], step
        ).wait()
        self.v_sum[step] = own[...] + self.v_land[step]
        if step < 4:
            self.vec_go(step + 1)


    def tick(self, name, step=None):
        for action, at in self.table.get(name, ()):
            if at is None or isinstance(step, int):
                if at is None or at == step:
                    self.act(action)
            else:
                pl.when(step == at)(functools.partial(self.act, action))

    def act(self, action):
        verb, name = action
        if verb == SEND:
            self.go(name, 0)
        elif verb == FREE:
            for other in name:
                self.travel(other, 0).wait_send()
                self.gone.add((other, 0))
            if name == MIDDLE:
                for other in INS:
                    self.allow(other, ORDER[other][0])
            else:
                for other in MIDDLE if name == REDUCES else (S_OUT, *INS):
                    self.allow(other, FEAT)
        elif verb == GO:
            self.go(name, 1)
        elif verb == BEGIN:
            for copy in self.copies_out(name):
                copy.start()
        elif verb == REUSE:
            near, far = self.copies_out(name)
            near.wait()
            far.wait_send()
        else:
            self.step(name, verb)

    def run(self):
        self.table, self.gone = {}, set()
        for name, at, actions in SCHEDULE:
            self.table.setdefault(name, []).extend((action, at) for action in actions)
        self.where_am_i()
        self.exchange()
        for copy in self.own:
            copy.start()
        self.start_weights()
        place = self.gs_half.at[self.feat]
        place[0:3, :] = self.gains[...]
        place[3:6, :] = self.shifts[...]
        self.greet()
        for copy in self.sent:
            copy.start()
        self.prepare()
        self.vec[...] = jnp.zeros(self.vec.shape, F32)
        self.landed(3)
        self.gs[...] = jnp.concatenate([self.gs_half[0], self.gs_half[1]], axis=1)
        self.landed(0)
        self.x[...] = self.x_t[...].T
        self.phases()
        self.act((BEGIN, INPUT_GRAD))
        self.v_half[0] = self.vec[:, : self.width // 2]
        self.v_half[1] = pltpu.roll(self.vec[...], self.width // 2, 1)[:, : self.width // 2]
        self.vec_go(0)
        for step in range(5):
            self.tick(END, step)
            self.vec_step(step)
        self.tick(END, 5)
        self.o_gain[...] = self.v_sum[4][0:3]
        self.o_shift[...] = self.v_sum[4][3:6]
        for name in PIECES:
            for step in range(5):
                if (name, step) not in self.gone:
                    self.travel(name, step).wait_send()
        for name in (LAYER_OUT, ENCODER_GRAD, INPUT_GRAD):
            if name != LAYER_OUT:
                self.act((REUSE, name))
            self.copies_out(name, local=False)[0].wait_recv()


def takes(step, *names):
    return tuple((step, name) for name in names)


SCHEDULE = (
    (FFN, 0, takes(SEND, EXPAND0)),
    (FFN, 1, takes(SEND, EXPAND1) + takes(0, EXPAND0)),
    (FFN, 2, takes(GO, EXPAND0) + takes(SEND, EXPAND2) + takes(0, EXPAND1)),
    (FFN_END, None, takes(SEND, REDUCE0, REDUCE1)),
    (NORM_3, 0, takes(GO, EXPAND1) + takes(0, EXPAND2, REDUCE0)),
    (NORM_3, 1, takes(GO, EXPAND2, REDUCE0) + takes(0, REDUCE1) + takes(BEGIN, LAYER_OUT)),
    (CROSS_START, None, takes(GO, REDUCE1) + takes(FREE, REDUCES, EXPANDS)),
    (MIXED, None, takes(SEND, S_MIX)),
    (KV, None, takes(SEND, S_KV) + takes(0, S_MIX) + takes(1, REDUCE0, REDUCE1) + takes(GO, S_MIX)),
    (NORM_2, 0, takes(0, S_KV)),
    (NORM_2, 1, takes(GO, S_KV) + takes(FREE, MIDDLE) + takes(BEGIN, ENCODER_GRAD) + takes(REUSE, LAYER_OUT)),
    (SELF_START, None, takes(SEND, S_OUT) + takes(1, *EXPANDS)),
    (SELF, 0, takes(0, S_OUT)),
    (SELF, 1, takes(GO, S_OUT)),
    (SELF, 3, takes(1, S_MIX)),
    (IN, 0, takes(SEND, S_IN0)),
    (IN, 1, takes(SEND, S_IN1) + takes(0, S_IN0) + takes(GO, S_IN0)),
    (IN, 2, takes(SEND, S_IN2) + takes(0, S_IN1) + takes(GO, S_IN1)),
    (IN, 2, takes(2, REDUCE0, REDUCE1) + takes(0, S_IN2) + takes(GO, S_IN2)),
    (NORM_1, 0, takes(1, S_KV, S_OUT) + takes(2, *EXPANDS)),
    (NORM_1, 1, takes(2, S_MIX) + takes(3, REDUCE0, REDUCE1)),
    (END, 1, takes(1, *INS) + takes(3, *EXPANDS)),
    (END, 2, takes(3, S_MIX) + takes(2, S_OUT)),
    (END, 3, takes(2, S_IN0, S_IN1, S_IN2, S_KV) + takes(4, REDUCE0, REDUCE1)),
    (END, 4, takes(3, S_OUT, S_KV, *INS) + takes(4, S_MIX, *EXPANDS)),
    (END, 5, takes(4, S_OUT, S_KV, *INS)),
)


def spaces():
    return tuple(pl.BlockSpec(memory_space=s) for s in (pltpu.VMEM, pl.ANY, pltpu.SMEM))


def spill_outs(rows, hbm):
    return {
        f"spill{b}": (jax.ShapeDtypeStruct((HEADS, kn, qn), BF16), hbm)
        for b, (_, qn, _, kn) in enumerate(self_blocks(rows))
    }


COST = pl.CostEstimate(flops=50 * 10**9, bytes_accessed=40 * 10**6, transcendentals=0)


def local_layer(x, enc, og, t_len, s_len, gs, weights):
    rows, width = x.shape
    hidden = weights[5].shape[1]
    vmem, hbm, smem = spaces()
    shape = jax.ShapeDtypeStruct
    ins = dict(x=x, enc=enc, og=og, t_len=t_len, s_len=s_len, gs=gs)
    whole, pairs = shape((rows, width), F32), lambda n: (shape((2, width, n), BF16), hbm)
    outs = dict(
        layer_out=(whole, vmem),
        mid2=(whole, vmem),
        encoder_grad=(shape((rows, width), BF16), vmem),
        vec=(shape((8, width), F32), vmem),
        s_reduce=(shape((2, hidden // 2, width), BF16), vmem),
        s_expand=(shape((2, width, hidden // 2), BF16), vmem),
        to_kv=pairs(LANES[S_KV]),
        to_mix=pairs(LANES[S_MIX]),
        to_out=pairs(LANES[S_OUT]),
        to_in0=pairs(LANES[S_IN0]),
        to_in1=pairs(LANES[S_IN1]),
        to_in2=pairs(LANES[S_IN2]),
        **spill_outs(rows, hbm),
    )
    scratch = dict(scratch_of(rows, width, hidden), s_sem=pltpu.SemaphoreType.DMA((12,)))

    def kernel(*refs):
        first, rest = refs[: len(ins)], refs[len(ins) + 7 :]
        named = dict(zip(list(ins) + list(outs) + list(scratch), first + rest))
        LocalLayer(**share(sources=refs[len(ins) : len(ins) + 7], **named)).run()

    found = pl.pallas_call(
        kernel,
        out_shape=[o[0] for o in outs.values()],
        in_specs=[vmem, vmem, vmem, smem, smem, vmem] + [hbm] * 7,
        out_specs=[o[1] for o in outs.values()],
        scratch_shapes=list(scratch.values()),
        compiler_params=pltpu.CompilerParams(vmem_limit_bytes=VMEM_LIMIT),
        cost_estimate=COST,
    )(*ins.values(), *weights)
    return dict(zip(outs, found))


def whole_layer(inputs, encoder, output_grad, t_len, s_len, gains, shifts, weights):
    rows, half = inputs.shape[1] // 2, inputs.shape[0]
    width, hidden = 2 * half, weights[5].shape[1]
    shard = width // 16
    vmem, hbm, smem = spaces()
    shape = jax.ShapeDtypeStruct
    ins = dict(x_in=inputs, e_in=encoder, g_in=output_grad, t_len=t_len, s_len=s_len)
    ins.update(gains=gains, shifts=shifts)
    big, small = (shape(inputs.shape, F32), hbm), lambda *dims: (shape(dims, F32), vmem)
    outs = dict(
        layer_out=big,
        input_grad=big,
        encoder_grad=big,
        o_gain=small(3, half),
        o_shift=small(3, half),
        o_in=small(shard, 3 * half),
        o_out=small(shard, half),
        o_cq=small(shard, half),
        o_kv=small(shard, width),
        o_co=small(shard, half),
        o_expand=small(shard, hidden // 2),
        o_reduce=small(hidden // 16, half),
    )
    count = len(outs)
    outs.update(spill_outs(rows, hbm))
    vm, pieces = pltpu.VMEM, len(PIECES)
    dma, regular = pltpu.SemaphoreType.DMA, pltpu.SemaphoreType.REGULAR
    scratch = dict(
        scratch_of(rows, width, hidden),
        x=vm((rows, width), F32),
        gs=vm((8, width), F32),
        vec=vm((8, width), F32),
        mid2=vm((rows, width), F32),
        x_t=vm((width, rows), F32),
        grad_t=vm((width, rows), F32),
        e_t=vm((width, rows), BF16),
        gs_half=vm((2, 8, half), F32),
        s_reduce=vm((2, hidden // 2, width), BF16),
        s_expand=vm((2, width, hidden // 2), BF16),
        l_reduce=vm((hidden // 2, width), BF16),
        l_expand=vm((width, hidden // 2), BF16),
        v_half=vm((2, 8, half), F32),
        v_sum=vm((5, 8, half), F32),
        v_land=vm((5, 8, half), F32),
        in_own=dma((3,)),
        in_send=dma((4,)),
        in_recv=dma((4,)),
        out_own=dma((3,)),
        out_send=dma((3,)),
        out_recv=dma((3,)),
        send_sem=dma((pieces + 1, 5)),
        recv_sem=dma((pieces + 1, 5)),
        credit=regular((pieces, 4)),
    )
    ends = []
    for name in PIECES:
        dims = (shard, EXPAND_LANES if name in EXPANDS else LANES.get(name))
        dims = (hidden // 32, half) if name in REDUCES else dims
        ends += [vm(dims, F32), vm(dims, BF16), vm(dims, BF16)]

    def kernel(*refs):
        first, rest = refs[: len(ins)], refs[len(ins) + 7 :]
        names = list(ins) + list(outs) + list(scratch)
        last = rest[len(outs) + len(scratch) :]
        named = dict(zip(names, first + rest))
        named.update(z_keep=last[0::3], z_send=last[1::3], z_land=last[2::3])
        RemoteLayer(**share(sources=refs[len(ins) : len(ins) + 7], **named)).run()

    found = pl.pallas_call(
        kernel,
        out_shape=[o[0] for o in outs.values()],
        in_specs=[hbm, hbm, hbm, smem, smem, vmem, vmem] + [hbm] * 7,
        out_specs=[o[1] for o in outs.values()],
        scratch_shapes=list(scratch.values()) + ends,
        compiler_params=pltpu.CompilerParams(
            vmem_limit_bytes=VMEM_LIMIT, collective_id=0, has_side_effects=True
        ),
        cost_estimate=COST,
    )(*ins.values(), *weights)
    return found[:count]


def hand_over(*arrays):
    count = len(arrays)

    def kernel(*refs):
        sources, targets, middle = (refs[n * count : (n + 1) * count] for n in range(3))
        before, after = refs[-2], refs[-1]
        comes = [pltpu.make_async_copy(sources[n], middle[n], before.at[n]) for n in range(count)]
        goes = [pltpu.make_async_copy(middle[n], targets[n], after.at[n]) for n in range(count)]
        for copy in comes:
            copy.start()
        for come, go in zip(comes, goes):
            come.wait()
            go.start()
        for copy in goes:
            copy.wait()

    _, hbm, _ = spaces()
    sems = [pltpu.SemaphoreType.DMA((count,))] * 2
    return pl.pallas_call(
        kernel,
        out_shape=[jax.ShapeDtypeStruct(a.shape, a.dtype) for a in arrays],
        in_specs=[hbm] * count,
        out_specs=[hbm] * count,
        scratch_shapes=[pltpu.VMEM(a.shape, a.dtype) for a in arrays] + sems,
        compiler_params=pltpu.CompilerParams(vmem_limit_bytes=VMEM_LIMIT),
    )(*arrays)


def gather_rows(part):
    return lax.all_to_all(part, "feat", split_axis=0, concat_axis=1, tiled=True)


def spread_rows(part):
    return lax.all_to_all(part, "feat", split_axis=1, concat_axis=0, tiled=True)


def over_feat(staged):
    return lax.psum_scatter(staged, "feat", scatter_dimension=0, tiled=True)[0]


def over_dp(part):
    return lax.psum_scatter(part, "dp", scatter_dimension=0, tiled=True).astype(F32)


def by_collectives(
    inputs, encoder, output_grad, target_lengths, source_lengths, gains, shifts, *weights
):
    width = weights[1].shape[0]
    half = width // 2
    vectors = jnp.concatenate([gains, shifts, jnp.zeros_like(gains[:2])], axis=0)
    vectors = lax.all_gather(vectors, "feat", axis=1, tiled=True)
    got = local_layer(
        gather_rows(inputs),
        gather_rows(encoder),
        gather_rows(output_grad),
        target_lengths,
        source_lengths,
        vectors,
        weights,
    )
    first = lax.axis_index("feat") == 0
    vec = lax.psum(got["vec"], ("dp", "feat"))
    vec = jnp.where(first, vec[:, :half], vec[:, half:])
    red = over_feat(got["s_reduce"])
    reduce_grad = over_dp(jnp.concatenate([red[:, :half], red[:, half:]], axis=0))
    expand_grad = over_dp(over_feat(got["s_expand"]))
    kv_grad = over_dp(over_feat(got["to_kv"]))
    mix = over_dp(over_feat(got["to_mix"]))
    out_grad = over_dp(over_feat(got["to_out"]))[:, :half]
    parts = [got["to_in0"], got["to_in1"], got["to_in2"]]
    wide = over_dp(over_feat(jnp.concatenate(parts, axis=2)))
    low, high = wide[:, : 3 * half], jnp.concatenate([wide[:, 896:960], wide[:, :896]], axis=1)
    return (
        spread_rows(got["layer_out"]),
        spread_rows(got["mid2"]),
        spread_rows(got["encoder_grad"]).astype(F32),
        vec[:3],
        vec[3:6],
        jnp.where(first, low, high),
        out_grad,
        mix[:, half:],
        kv_grad,
        mix[:, :half],
        expand_grad,
        reduce_grad,
    )


def by_remote_copies(
    inputs, encoder, output_grad, target_lengths, source_lengths, gains, shifts, *weights
):
    got = whole_layer(
        inputs.T, encoder.T, output_grad.T, target_lengths, source_lengths, gains, shifts, weights
    )
    got = hand_over(*got)
    return tuple(part.T for part in got[:3]) + tuple(got[3:])


def solution(mesh):
    rows, both = P("dp", "feat"), P(("dp", "feat"), None)
    columns, whole = P(None, "feat"), P()
    small = mesh.shape["dp"] == 16 and mesh.shape["feat"] == 2
    return jax.shard_map(
        by_remote_copies if small else by_collectives,
        mesh=mesh,
        in_specs=(rows, rows, rows, both, both, columns, columns) + (whole,) * 7,
        out_specs=(rows, rows, rows, columns, columns) + (rows,) * 7,
        check_vma=False,
    )
```

```python
import functools
import math

import jax
import jax.numpy as jnp
from jax import lax
from jax.experimental import pallas as pl
from jax.experimental.pallas import tpu as pltpu
from jax.sharding import PartitionSpec as P

HEADS = 8
LONGEST = 256
EPSILON = 1e-05
MASKED = -1e30
F32 = jnp.float32
BF16 = jnp.bfloat16
WINDOW = 256
HIDDEN_TILE = 512
EXPAND_LANES = 512
W_IN, W_OUT, W_CQ, W_KV, W_CO, W_EXPAND, W_REDUCE, W_IN_AGAIN = range(8)
FFN, FFN_END, NORM_3, CROSS_START, CROSS, MIXED, KV, NORM_2, SELF_START, SELF, IN, NORM_1, END = range(13)
EXPAND0, EXPAND1, EXPAND2, REDUCE0, REDUCE1, S_MIX, S_KV, S_OUT, S_IN0, S_IN1, S_IN2 = PIECES = range(11)
EXPANDS, REDUCES = (EXPAND0, EXPAND1, EXPAND2), (REDUCE0, REDUCE1)
INS, MIDDLE = (S_IN0, S_IN1, S_IN2), (S_MIX, S_KV)
FEAT, X, Y, Z1, Z2 = range(5)
QUERY_BLOCKS = ((0, 256), (256, 256), (512, 128))
VMEM_LIMIT = 65_000 * 2**10


def nn(left, right):
    return lax.dot_general(left, right, (((1,), (0,)), ((), ())), preferred_element_type=F32)


def nt(left, right):
    return lax.dot_general(left, right, (((1,), (1,)), ((), ())), preferred_element_type=F32)


def self_blocks(rows):
    found = []
    for start, size in QUERY_BLOCKS:
        first = max(0, start - LONGEST)
        found.append((start, size, first, start + size - first))
    return found


def cross_blocks(rows):
    return [(start, size, 0, min(rows, start + size + LONGEST)) for start, size in QUERY_BLOCKS]


def gelu_parts(value):
    root = math.sqrt(2.0 / math.pi)
    square = value * value
    inner = value * (root + (root * 0.044715) * square)
    bent = jnp.tanh(inner)
    up = 0.5 + 0.5 * bent
    slope = (0.5 * value) * (1.0 - bent * bent) * (root + (3.0 * root * 0.044715) * square)
    return value * up, up + slope


def norm_stats(value):
    mean = jnp.mean(value, axis=1, keepdims=True)
    second = jnp.mean(value * value, axis=1, keepdims=True)
    scale = lax.rsqrt(second - mean * mean + EPSILON)
    return (value - mean) * scale, scale


def pack_halves(left, right):
    width = left.shape[1]
    low = lax.broadcasted_iota(jnp.int32, left.shape, 1) < width // 2
    return (
        jnp.where(low, left, pltpu.roll(right, width // 2, 1)),
        jnp.where(low, pltpu.roll(left, width // 2, 1), right),
    )


def in_spans(width):
    half, part = 3 * width // 2, 384
    high = half + 64
    yield S_IN0, ((0, part), (high, part))
    yield S_IN1, ((part, part), (high + part, part))
    yield S_IN2, ((2 * part, 256), (high + 2 * part, 128))


class Layer:
    def __init__(self, **refs):
        self.__dict__.update(refs)
        self.rows, self.width = self.branch1.shape
        self.hidden = self.w_expand.shape[1]
        self.head = self.width // HEADS
        most = -(-self.rows // 256) * 128
        self.halves = [(0, most), (most, self.rows - most)]


    def segments(self, lengths, shape, axis):
        place = lax.broadcasted_iota(jnp.int32, shape, axis)
        found = jnp.zeros(shape, jnp.int32)
        end = jnp.int32(0)
        for slot in range(lengths.shape[1]):
            end = end + lengths[0, slot]
            found = found + jnp.where(place >= end, 1, 0)
        return found, place < end, place

    def prepare(self):
        rows = self.rows
        lane = lax.broadcasted_iota(jnp.int32, (rows, 128), 1)
        columns = []
        for lengths in (self.t_len, self.s_len):
            seg, valid, _ = self.segments(lengths, (rows, 128), 0)
            columns.append(jnp.where(valid, seg, -2))
        self.t_col[...] = jnp.where(lane < 64, *columns)
        seg, valid, _ = self.segments(self.t_len, (8, rows), 1)
        self.t_row[...] = jnp.where(valid, seg, -1)

    def kept(self, part):
        return jnp.where(self.t_col[part, 0:1] >= 0, 1.0, 0.0).astype(F32)

    def make_bias(self, blocks, lane, causal):
        for ref, (q0, qn, k0, kn) in zip(self.bias, blocks):
            allowed = self.t_col[k0 : k0 + kn, lane : lane + 1] == self.t_row[0:1, q0 : q0 + qn]
            if causal:
                key = lax.broadcasted_iota(jnp.int32, (kn, qn), 0) + k0
                query = lax.broadcasted_iota(jnp.int32, (kn, qn), 1) + q0
                allowed = allowed & (key <= query)
            ref[0:kn, :] = jnp.where(allowed, 0.0, MASKED).astype(F32)


    def window(self, head):
        tiles = jnp.minimum((head * self.head) // 128, (self.width - WINDOW) // 128)
        start = pl.multiple_of(tiles * 128, 128)
        lane = lax.broadcasted_iota(jnp.int32, (8, WINDOW), 1) + start
        mine = (lane >= head * self.head) & (lane < (head + 1) * self.head)
        return start, jnp.where(mine, 1.0, 0.0).astype(F32)[0:1]

    def attend(self, queries, q_at, keys, k_at, mixed_t, blocks):
        factor = math.log2(math.e) / math.sqrt(self.head)

        @pl.loop(0, HEADS, unroll=2)
        def _(head):
            start, mine = self.window(head)
            band = pl.ds(pl.multiple_of(head * self.head, 16), self.head)
            for b, (q0, qn, k0, kn) in enumerate(blocks):
                query = queries[q0 : q0 + qn, pl.ds(q_at + start, WINDOW)]
                query = (query.astype(F32) * mine).astype(BF16)
                key = keys[k0 : k0 + kn, pl.ds(k_at + start, WINDOW)]
                scores = nt(key, query) + self.bias[b][0:kn, :]
                largest = jnp.max(scores, axis=0, keepdims=True)
                expo = jnp.exp2((scores - largest) * factor)
                total = jnp.sum(expo, axis=0, keepdims=True)
                weights = (expo * (1.0 / total)).astype(BF16)
                self.p[b][head, 0:kn, :] = weights
                mixed = nn(self.v_t[band, k0 : k0 + kn], weights)
                mixed_t[band, q0 : q0 + qn] = mixed.astype(BF16)

    def attend_back(self, queries, q_at, keys, k_at, values, v_at, mixed_t, blocks, name):
        scale = 1.0 / math.sqrt(self.head)
        self.dk[...] = jnp.zeros(self.dk.shape, F32)
        self.dv[...] = jnp.zeros(self.dv.shape, F32)

        @pl.loop(0, HEADS // 2)
        def _(pair):
            for head in (2 * pair, 2 * pair + 1):
                start, mine = self.window(head)
                band = pl.ds(pl.multiple_of(head * self.head, 16), self.head)
                lanes = pl.ds(start, WINDOW)
                for b, (q0, qn, k0, kn) in enumerate(blocks):
                    query = queries[q0 : q0 + qn, pl.ds(q_at + start, WINDOW)]
                    query = (query.astype(F32) * mine).astype(BF16)
                    grad = (self.g[q0 : q0 + qn, lanes].astype(F32) * mine).astype(BF16)
                    value = values[k0 : k0 + kn, pl.ds(v_at + start, WINDOW)]
                    weights = self.p[b][head, 0:kn, :]
                    product = self.g_t[band, q0 : q0 + qn].astype(F32) * mixed_t[band, q0 : q0 + qn].astype(F32)
                    centre = jnp.sum(product, axis=0, keepdims=True)
                    grad_w = nt(value, grad)
                    grad_s = (weights.astype(F32) * (grad_w - centre)).astype(BF16)
                    self.dv[k0 : k0 + kn, lanes] += nn(weights, grad)
                    self.dk[k0 : k0 + kn, lanes] += nn(grad_s, query)
                    grad_q = nn(self.k_t[band, k0 : k0 + kn], grad_s)
                    self.dq_t[band, q0 : q0 + qn] = (grad_q * scale).astype(BF16)
            self.tick(name, pair)


    def norm_to(self, value, which, start, size, target):
        normed, _ = norm_stats(value)
        gain, shift = self.gs[which : which + 1, :], self.gs[3 + which : 4 + which, :]
        target[start : start + size, :] = (normed * gain + shift).astype(BF16)

    def norm_back(self, grad, value, which, first):
        normed, scale = norm_stats(value)
        scaled = grad * self.gs[which : which + 1, :]
        one = jnp.mean(scaled, axis=1, keepdims=True)
        two = jnp.mean(scaled * normed, axis=1, keepdims=True)
        gain = jnp.sum(grad * normed, axis=0, keepdims=True)
        shift = jnp.sum(grad, axis=0, keepdims=True)
        if first:
            self.vec[which : which + 1, :] = gain
            self.vec[3 + which : 4 + which, :] = shift
        else:
            self.vec[which : which + 1, :] += gain
            self.vec[3 + which : 4 + which, :] += shift
        return (scaled - one - normed * two) * scale


    def forward_self(self):
        width = self.width
        for start, size in self.halves:
            part = slice(start, start + size)
            self.norm_to(self.x[part, :], 0, start, size, self.g)
        self.arrive(W_IN)
        for col in range(0, 3 * width, width):
            self.proj[:, col : col + width] = nn(
                self.g[...], self.w_in[:, col : col + width]
            ).astype(BF16)
        self.v_t[...] = self.proj[:, 2 * width :].T
        self.make_bias(self_blocks(self.rows), 0, True)
        self.attend(self.proj, 0, self.proj, width, self.mixed1_t, self_blocks(self.rows))

    def forward_cross(self):
        width = self.width
        self.spill_weights()
        self.arrive(W_KV)
        enc = self.encoder_rows(self.k_t)
        for col in range(0, 2 * width, width):
            self.memory[:, col : col + width] = nn(
                enc[...], self.w_kv[:, col : col + width]
            ).astype(BF16)
        self.v_t[...] = self.memory[:, width:].T
        self.g[...] = self.mixed1_t[...].T
        self.arrive(W_OUT)
        self.arrive(W_CQ)
        for start, size in self.halves:
            part = slice(start, start + size)
            branch = (nn(self.g[part, :], self.w_out[...]) * self.kept(part)).astype(BF16)
            mid = self.x[part, :] + branch.astype(F32)
            self.branch1[part, :] = branch
            self.norm_to(mid, 1, start, size, self.normed2)
            self.cq[part, :] = nn(self.normed2[part, :], self.w_cq[...]).astype(BF16)
        self.make_bias(cross_blocks(self.rows), 64, False)
        self.spill_wait()
        self.attend(self.cq, 0, self.memory, 0, self.mixed2_t, cross_blocks(self.rows))

    def mid1_rows(self, part):
        return self.x[part, :] + self.branch1[part, :].astype(F32)

    def feed_forward(self):
        width, tile = self.width, HIDDEN_TILE
        self.g[...] = self.mixed2_t[...].T
        self.arrive(W_CO)
        for start, size in self.halves:
            part = slice(start, start + size)
            branch = (nn(self.g[part, :], self.w_co[...]) * self.kept(part)).astype(BF16)
            mid = self.mid1_rows(part) + branch.astype(F32)
            self.mid2[part, :] = mid
            self.norm_to(mid, 2, start, size, self.normed3)
        self.k_t[...] = self.normed3[...].T
        self.landed(2)
        for start, size in self.halves:
            part = slice(start, start + size)
            self.g[part, :] = (self.grad_rows(part) * self.kept(part)).astype(BF16)
        self.dk[...] = jnp.zeros(self.dk.shape, F32)
        self.dv[...] = jnp.zeros(self.dv.shape, F32)
        self.arrive(W_EXPAND)
        self.arrive(W_REDUCE)

        @pl.loop(0, self.hidden // (2 * tile))
        def _(step):
            actives = []
            low = pl.multiple_of(step * tile, tile)
            for side in range(2):
                at = pl.multiple_of(side * (self.hidden // 2) + step * tile, tile)
                expand = self.w_expand[:, pl.ds(at, tile)]
                reduce = self.w_reduce[pl.ds(at, tile), :]
                value = nn(self.normed3[...], expand).astype(BF16).astype(F32)
                active, slope = gelu_parts(value)
                active = active.astype(BF16)
                grad = (nt(self.g[...], reduce) * slope).astype(BF16)
                self.dk[...] += nn(active, reduce)
                self.dv[...] += nt(grad, expand)
                self.put_expand(step, side, low, nn(self.k_t[...], grad))
                actives.append(active)
            for part in range(0, tile, 256):
                sides = [nn(active[:, part : part + 256].T, self.g[...]) for active in actives]
                for side, packed in enumerate(pack_halves(*sides)):
                    self.put_reduce(step * (tile // 256) + part // 256, side, low + part, packed)
            self.tick(FFN, step)

        self.tick(FFN_END)
        for n, (start, size) in enumerate(self.halves):
            part = slice(start, start + size)
            mid = self.mid2[part, :]
            branch = (self.dk[part, :] * self.kept(part)).astype(BF16)
            self.put_layer_out(part, mid + branch.astype(F32))
            grad = self.dv[part, :].astype(BF16).astype(F32)
            self.mid2[part, :] = self.grad_rows(part) + self.norm_back(grad, mid, 2, n == 0)
            self.tick(NORM_3, n)

    def backward_cross(self):
        width = self.width
        self.mid_grad[...] = (self.mid2[...] * self.kept(slice(None))).astype(BF16)
        self.g[...] = nt(self.mid_grad[...], self.w_co[...]).astype(BF16)
        self.g_t[...] = self.g[...].T
        self.k_t[...] = self.memory[:, 0:width].T
        self.tick(CROSS_START)
        self.attend_back(
            self.cq, 0, self.memory, 0, self.memory, width, self.mixed2_t, cross_blocks(self.rows), CROSS
        )
        self.refetch()
        out_grad = nn(self.mixed2_t[...], self.mid_grad[...])
        self.fetch_weights()
        scale = 1.0 / math.sqrt(self.head)
        self.gmem[:, 0:width] = (self.dk[...] * scale).astype(BF16)
        self.gmem[:, width : 2 * width] = self.dv[...].astype(BF16)
        self.g[...] = self.dq_t[...].T
        self.k_t[...] = self.normed2[...].T
        for side, packed in enumerate(pack_halves(out_grad, nn(self.k_t[...], self.g[...]))):
            self.put_rows(S_MIX, side, packed)
        self.tick(MIXED)
        enc_t = self.encoder_columns(self.k_t)
        for side in range(2):
            self.put_rows(
                S_KV, side, nn(enc_t[...], self.gmem[:, side * width : (side + 1) * width])
            )
        self.tick(KV)
        for n, (start, size) in enumerate(self.halves):
            part = slice(start, start + size)
            self.put_encoder_grad(part, nt(self.gmem[part, 0 : 2 * width], self.w_kv[...]).astype(BF16))
            grad = nt(self.g[part, :], self.w_cq[...]).astype(BF16).astype(F32)
            self.mid2[part, :] += self.norm_back(grad, self.mid1_rows(part), 1, n == 0)
            self.tick(NORM_2, n)

    def backward_self(self):
        width = self.width
        self.mid_grad[...] = (self.mid2[...] * self.kept(slice(None))).astype(BF16)
        self.g[...] = nt(self.mid_grad[...], self.w_out[...]).astype(BF16)
        self.g_t[...] = self.g[...].T
        self.k_t[...] = self.proj[:, width : 2 * width].T
        self.put_rows_split(S_OUT, nn(self.mixed1_t[...], self.mid_grad[...]))
        self.fetch_wait()
        self.tick(SELF_START)
        self.attend_back(
            self.proj, 0, self.proj, width, self.proj, 2 * width, self.mixed1_t, self_blocks(self.rows), SELF
        )
        scale = 1.0 / math.sqrt(self.head)
        self.gmem[:, 0:width] = self.dq_t[...].T
        self.gmem[:, width : 2 * width] = (self.dk[...] * scale).astype(BF16)
        self.gmem[:, 2 * width :] = self.dv[...].astype(BF16)
        for start, size in self.halves:
            self.norm_to(self.x[start : start + size, :], 0, start, size, self.g)
        self.k_t[...] = self.g[...].T
        for n, (name, spans) in enumerate(in_spans(width)):
            for side, (col, size) in enumerate(spans):
                value = nn(self.k_t[...], self.gmem[:, col : col + size])
                if n == 2 and side == 1:
                    odd = nn(self.k_t[...], self.gmem[:, 896:1024])
                    value = jnp.concatenate([value, pltpu.roll(odd, 64, 1)], axis=1)
                self.put_rows(name, side, value)
            self.tick(IN, n)
        self.arrive(W_IN_AGAIN)
        for n, (start, size) in enumerate(self.halves):
            part = slice(start, start + size)
            grad = nt(self.gmem[part, :], self.w_in[...]).astype(BF16).astype(F32)
            self.put_input_grad(
                part, self.mid2[part, :] + self.norm_back(grad, self.x[part, :], 0, n == 0)
            )
            self.tick(NORM_1, n)


def scratch_of(rows, width, hidden):
    wide = [k[3] for k in cross_blocks(rows)]
    vm = pltpu.VMEM
    named = dict(
        w_in=vm((width, 3 * width), BF16),
        w_out=vm((width, width), BF16),
        w_cq=vm((width, width), BF16),
        w_kv=vm((width, 2 * width), BF16),
        w_co=vm((width, width), BF16),
        w_expand=vm((width, hidden), BF16),
        w_reduce=vm((hidden, width), BF16),
        t_col=vm((rows, 128), jnp.int32),
        t_row=vm((8, rows), jnp.int32),
        proj=vm((rows, 3 * width), BF16),
        v_t=vm((width, rows), BF16),
        mixed1_t=vm((width, rows), BF16),
        branch1=vm((rows, width), BF16),
        pair=vm((2, rows, width), BF16),
        normed3=vm((rows, width), BF16),
        g=vm((rows, width), BF16),
        k_t=vm((width, rows), BF16),
        dk=vm((rows, width), F32),
        dv=vm((rows, width), F32),
        w_sem=pltpu.SemaphoreType.DMA((7,)),
        p_sem=pltpu.SemaphoreType.DMA((3,)),
        again_sem=pltpu.SemaphoreType.DMA(()),
    )
    for b, (_, qn, _, kn) in enumerate(cross_blocks(rows)):
        named[f"p{b}"] = vm((HEADS, kn, qn), BF16)
    return named


class SavedLayer(Layer):
    def put_rows_split(self, name, value):
        turned = pltpu.roll(value, value.shape[1] // 2, 1)
        for side, part in enumerate((value, turned)):
            self.put_rows(name, side, part[:, : LANES[name]])

    def start_weights(self):
        targets = (self.w_in, self.w_out, self.w_cq, self.w_kv, self.w_co, self.w_expand, self.w_reduce)
        self.copies = {
            n: pltpu.make_async_copy(self.sources[n], target, self.w_sem.at[n])
            for n, target in enumerate(targets)
        }
        for copy in self.copies.values():
            copy.start()

    def refetch(self):
        self.copies[W_IN_AGAIN] = pltpu.make_async_copy(
            self.sources[W_IN], self.w_in, self.again_sem
        )
        self.copies[W_IN_AGAIN].start()

    def arrive(self, name):
        self.copies[name].wait()

    def spill_copies(self, back):
        found = []
        for b, (_, _, _, kn) in enumerate(self_blocks(self.rows)):
            here, there = self.p[b].at[:, 0:kn, :], self.spill[b]
            pair = (there, here) if back else (here, there)
            found.append(pltpu.make_async_copy(*pair, self.p_sem.at[b]))
        return found

    def spill_weights(self):
        for copy in self.spill_copies(False):
            copy.start()

    def spill_wait(self):
        for copy in self.spill_copies(False):
            copy.wait()

    def fetch_weights(self):
        for copy in self.spill_copies(True):
            copy.start()

    def fetch_wait(self):
        for copy in self.spill_copies(True):
            copy.wait()

    def phases(self):
        self.forward_self()
        self.forward_cross()
        self.feed_forward()
        self.backward_cross()
        self.backward_self()


def share(p0, p1, p2, spill0, spill1, spill2, sources, pair, **named):
    rows, width = named["branch1"].shape
    first, expand, reduce, proj = (named[n] for n in ("w_in", "w_expand", "w_reduce", "proj"))

    def place(name, side):
        if name in (S_KV, S_MIX):
            at = side * width + (2 * width if name == S_MIX else 0)
            return reduce, pl.multiple_of(at, width), 0
        if name == S_OUT:
            return pair.at[side], 0, 0
        if name == S_IN2:
            return expand, 0, pl.multiple_of(4 * width + side * 256, 128)
        at = side * 768 + (384 if name == S_IN1 else 0)
        return proj, 0, pl.multiple_of(at, 128)

    return dict(
        named,
        g_t=named["v_t"],
        dq_t=named["normed3"],
        memory=first.at[:, 0 : 2 * width],
        cq=first.at[:, 2 * width : 3 * width],
        gmem=expand.at[:, 0 : 3 * width],
        mid_grad=expand.at[:, 3 * width : 4 * width],
        bias=[named["dk"].at[0:kn, q0 : q0 + qn] for q0, qn, _, kn in cross_blocks(rows)],
        p=(p0, p1, p2),
        spill=(spill0, spill1, spill2),
        sources=sources,
        normed2=pair.at[0],
        mixed2_t=pair.at[1],
        place=place,
    )


LANES = {S_MIX: 640, S_KV: 640, S_OUT: 384, S_IN0: 384, S_IN1: 384, S_IN2: 256}


class LocalLayer(SavedLayer):
    def staged(self, names):
        targets = {S_KV: self.to_kv, S_MIX: self.to_mix, S_OUT: self.to_out}
        targets.update({S_IN0: self.to_in0, S_IN1: self.to_in1, S_IN2: self.to_in2})
        found = []
        for name in names:
            for side in range(2):
                base, row, col = self.place(name, side)
                found.append(
                    pltpu.make_async_copy(
                        base.at[pl.ds(row, self.width), pl.ds(col, LANES[name])],
                        targets[name].at[side],
                        self.s_sem.at[2 * (name - S_MIX) + side],
                    )
                )
        return found

    def tick(self, name, step=None):
        for when, pieces in ((KV, (S_MIX, S_KV)), (SELF_START, (S_OUT,)), (NORM_1, (S_IN0, S_IN1, S_IN2))):
            if name == when and step in (None, 0):
                for copy in self.staged(pieces):
                    copy.start()

    def encoder_columns(self, spare):
        spare[...] = self.enc[...].T
        return spare

    def encoder_rows(self, spare):
        return self.enc

    def landed(self, n):
        pass

    def grad_rows(self, part):
        return self.og[part, :]

    def put_rows(self, name, side, value):
        base, row, col = self.place(name, side)
        base[pl.ds(row, self.width), pl.ds(col, value.shape[1])] = value.astype(BF16)

    def put_expand(self, step, side, low, value):
        self.s_expand[side, :, pl.ds(low, value.shape[1])] = value.astype(BF16)

    def put_reduce(self, step, side, low, value):
        self.s_reduce[side, pl.ds(low, value.shape[0]), :] = value.astype(BF16)

    def put_layer_out(self, part, value):
        self.layer_out[part, :] = value

    def put_input_grad(self, part, value):
        self.mid2[part, :] = value

    def put_encoder_grad(self, part, value):
        self.encoder_grad[part, :] = value

    def run(self):
        self.start_weights()
        self.prepare()
        self.vec[...] = jnp.zeros(self.vec.shape, F32)
        self.phases()
        for copy in self.staged((S_MIX, S_KV, S_OUT, S_IN0, S_IN1, S_IN2)):
            copy.wait()


MESH = pl.DeviceIdType.MESH
LAYER_OUT, ENCODER_GRAD, INPUT_GRAD = range(3)
SEND, FREE, BEGIN, REUSE, GO = range(5, 10)
ORDER = {
    EXPAND0: (Z1, X, Y),
    EXPAND1: (Z1, Y, X),
    EXPAND2: (Z1, X, Y),
    REDUCE0: (Y, X, Z1),
    REDUCE1: (X, Y, Z1),
    S_MIX: (Z1, Y, X),
    S_KV: (X, Y, Z1),
    S_OUT: (Z1, Y, X),
    S_IN0: (X, Y, Z1),
    S_IN1: (Y, X, Z1),
    S_IN2: (Z1, X, Y),
}


class RemoteLayer(SavedLayer):
    def where_am_i(self):
        self.dp, self.feat = lax.axis_index("dp"), lax.axis_index("feat")
        bits = [lax.rem(lax.div(self.dp, 1 << n), 2) for n in range(4)]
        self.bit = dict(zip((X, Y, Z1, Z2), bits))
        self.peer = {FEAT: (self.dp, 1 - self.feat)}
        for n, link in enumerate((X, Y, Z1, Z2)):
            self.peer[link] = (self.dp + (1 << n) * (1 - 2 * bits[n]), self.feat)

    def remote(self, source, target, send, receive, link):
        return pltpu.make_async_remote_copy(
            source, target, send, receive, device_id=self.peer[link], device_id_type=MESH
        )

    def greet(self):
        barrier = pltpu.get_barrier_semaphore()
        for link in range(5):
            pl.semaphore_signal(barrier, 1, device_id=self.peer[link], device_id_type=MESH)
        pl.semaphore_wait(barrier, 5)


    def mine(self, size):
        return pl.ds(pl.multiple_of(self.feat * size, size), size)

    def other(self, size):
        return pl.ds(pl.multiple_of((1 - self.feat) * size, size), size)

    def exchange(self):
        rows, half = self.rows, self.width // 2
        pairs = ((self.x_in, self.x_t), (self.e_in, self.e_t), (self.g_in, self.grad_t))
        self.own, self.sent = [], []
        for n, (source, target) in enumerate(pairs):
            place = target.at[self.mine(half), :]
            mine, other = source.at[:, self.mine(rows)], source.at[:, self.other(rows)]
            self.own.append(pltpu.make_async_copy(mine, place, self.in_own.at[n]))
            self.sent.append(self.remote(other, place, self.in_send.at[n], self.in_recv.at[n], FEAT))
        place = self.gs_half.at[self.feat]
        self.sent.append(self.remote(place, place, self.in_send.at[3], self.in_recv.at[3], FEAT))

    def landed(self, n):
        if n < 3:
            self.own[n].wait()
        self.sent[n].wait()

    def encoder_rows(self, spare):
        self.landed(1)
        spare[...] = self.e_t[...].T
        return spare

    def encoder_columns(self, spare):
        return self.e_t

    def grad_rows(self, part):
        return self.grad_t[:, part].T


    def copies_out(self, name, local=True):
        source = self.grad_t if name == ENCODER_GRAD else self.x_t
        half = self.width // 2
        place = (self.layer_out, self.encoder_grad, self.input_grad)[name].at[:, self.mine(self.rows)]
        far = self.remote(
            source.at[self.other(half), :], place, self.out_send.at[name], self.out_recv.at[name], FEAT
        )
        if not local:
            return (far,)
        near = pltpu.make_async_copy(source.at[self.mine(half), :], place, self.out_own.at[name])
        return near, far

    def put_layer_out(self, part, value):
        self.x_t[:, part] = value.T

    def put_encoder_grad(self, part, value):
        self.grad_t[:, part] = value.astype(F32).T

    def put_input_grad(self, part, value):
        self.x_t[:, part] = value.T


    def spot(self, name, side, row, count):
        if name in EXPANDS:
            lanes = pl.ds(EXPAND_LANES * (name - EXPAND0), EXPAND_LANES)
            return self.s_expand.at[side, pl.ds(row, count), lanes]
        if name in REDUCES:
            height = self.s_reduce.shape[1] // 2
            return self.s_reduce.at[side, pl.ds((name - REDUCE0) * height + row, count), :]
        base, top, left = self.place(name, side)
        return base.at[pl.ds(top + row, count), pl.ds(left, LANES[name])]

    def landing(self, name, side, row, count):
        if name in EXPANDS:
            lanes = pl.ds(EXPAND_LANES * (name - EXPAND0), EXPAND_LANES)
            return self.l_expand.at[pl.ds(row, count), lanes]
        if name in REDUCES:
            height = self.s_reduce.shape[1] // 2
            return self.l_reduce.at[pl.ds((name - REDUCE0) * height + row, count), :]
        if name in (S_KV, S_MIX):
            first = self.width if name == S_MIX else 0
            return self.s_reduce.at[side, pl.ds(first + row, count), :]
        return self.s_expand.at[side, pl.ds(row, count), pl.ds(384 * (name - S_OUT), LANES[name])]

    def landing_one(self, name, row, count):
        half = self.width // 2
        first = {S_IN0: 0, S_IN1: half, S_IN2: 2 * self.width}[name]
        at = pl.multiple_of((1 - self.feat) * self.width, self.width) + first + row
        return self.w_reduce.at[pl.ds(at, count), pl.ds(0, LANES[name])]

    def plan(self, name):
        quarter = (self.s_reduce.shape[1] // 2 if name in REDUCES else self.width) // 4
        links = ORDER[name]
        one = self.bit[links[0]] * 2 * quarter
        two = one + self.bit[links[1]] * quarter
        three = two + self.bit[links[2]] * (quarter // 2)
        return quarter, links, (one, two, three)

    def travel(self, name, step):
        n = name
        quarter, links, (one, two, _) = self.plan(name)
        here, there = self.feat, 1 - self.feat
        if step == 0:
            link, count = FEAT, 4 * quarter
            source = self.spot(name, there, 0, count)
            target = self.landing(name, here, 0, count)
        elif step == 1:
            link, count = links[0], 2 * quarter
            source = self.spot(name, here, (1 - self.bit[link]) * count, count)
            target = self.landing(name, there, 0, count)
            if name in INS:
                target = self.landing_one(name, 0, count)
        elif step == 2:
            link, count = links[1], quarter
            source = self.spot(name, here, one + (1 - self.bit[link]) * count, count)
            target = self.landing(name, there, 2 * quarter, count)
        elif step == 3:
            link, count = links[2], quarter // 2
            source = self.spot(name, here, two + (1 - self.bit[link]) * count, count)
            target = self.landing(name, there, 3 * quarter, count)
        else:
            link, source, target = Z2, self.z_send[n], self.z_land[n]
        return self.remote(source, target, self.send_sem.at[n, step], self.recv_sem.at[n, step], link)

    def credit_at(self, name, link):
        return self.credit.at[name, link]

    def allow(self, name, link):
        pl.semaphore_signal(self.credit_at(name, link), 1, device_id=self.peer[link], device_id_type=MESH)

    def go(self, name, step):
        link = (FEAT, *ORDER[name], Z2)[step]
        if step in (1, 2, 3) or (step == 0 and name >= S_MIX):
            pl.semaphore_wait(self.credit_at(name, link), 1)
        self.travel(name, step).start()

    def add(self, name, row, count, from_row, step):
        mine = self.spot(name, self.feat, row, count)
        if step == 1 and name in INS:
            came = self.landing_one(name, from_row, count)
        else:
            came = self.landing(name, 1 - self.feat, from_row, count)
        mine[...] = mine[...] + came[...]

    def step(self, name, step):
        n = name
        quarter, links, (one, two, three) = self.plan(name)
        self.travel(name, step).wait_recv()
        if step == 0:
            for n in range(4):
                self.add(name, n * quarter, quarter, n * quarter, step)
            for link in links[1:] if name in INS else links:
                self.allow(name, link)
        elif step == 1:
            out, kept = (1 - self.bit[links[1]]) * quarter, self.bit[links[1]] * quarter
            self.add(name, one + out, quarter, out, step)
            self.go(name, 2)
            self.add(name, one + kept, quarter, kept, step)
        elif step == 2:
            half = quarter // 2
            out, kept = (1 - self.bit[links[2]]) * half, self.bit[links[2]] * half
            self.add(name, two + out, half, 2 * quarter + out, step)
            self.go(name, 3)
            self.add(name, two + kept, half, 2 * quarter + kept, step)
        elif step == 3:
            half = quarter // 2
            value = self.spot(name, self.feat, three, half)[...].astype(F32)
            value = value + self.landing(name, 1 - self.feat, 3 * quarter, half)[...].astype(F32)
            if name in REDUCES:
                wide = self.width // 2
                low, high = value[:, :wide], pltpu.roll(value, wide, 1)[:, :wide]
            else:
                low, high = value[: half // 2], value[half // 2 :]
            first = self.bit[Z2] == 0
            self.z_keep[n][...] = jnp.where(first, low, high)
            self.z_send[n][...] = jnp.where(first, high, low).astype(BF16)
            self.go(name, 4)
        else:
            value = self.z_keep[n][...] + self.z_land[n][...].astype(F32)
            self.finish(name, value)

    def finish(self, name, value):
        half = self.width // 2
        if name in EXPANDS:
            at = EXPAND_LANES * (name - EXPAND0)
            self.o_expand[:, at : at + value.shape[1]] = value
        elif name in REDUCES:
            at = value.shape[0] * (name - REDUCE0)
            self.o_reduce[at : at + value.shape[0], :] = value
        elif name == S_KV:
            self.o_kv[...] = value
        elif name == S_MIX:
            self.o_co[...] = value[:, :half]
            self.o_cq[...] = pltpu.roll(value, half, 1)[:, :half]
        elif name == S_OUT:
            self.o_out[...] = value[:, :half]
        elif name != S_IN2:
            self.z_keep[name][...] = value
        else:
            parts = [self.z_keep[S_IN0][...], self.z_keep[S_IN1][...], value]
            wide = jnp.concatenate(parts, axis=1)
            lane = lax.broadcasted_iota(jnp.int32, wide.shape, 1)
            moved = pltpu.roll(wide, 64, 1)
            moved = jnp.where(lane < 64, pltpu.roll(wide, 1024 - 896, 1), moved)
            self.o_in[...] = jnp.where(self.feat == 0, wide, moved)[:, : 3 * half]

    def seat(self, name, block):
        bits = {Z1: block // 4, Y: block // 2 % 2, X: block % 2}
        a, b, c = (bits[link] for link in ORDER[name])
        return 4 * a + 2 * b + c

    def in_pairs(self, value):
        rows = value.shape[0] // 16
        for n in range(8):
            part = [value[at * rows : (at + 1) * rows] for at in (n, n + 8)]
            yield n, jnp.concatenate(part, axis=0).astype(BF16)

    def put_rows(self, name, side, value):
        base, top, left = self.place(name, side)
        for block, part in self.in_pairs(value):
            row, count = self.seat(name, block) * part.shape[0], part.shape[0]
            base[pl.ds(top + row, count), pl.ds(left, part.shape[1])] = part

    def put_expand(self, step, side, low, value):
        which = lax.div(step * value.shape[1], EXPAND_LANES)
        for block, part in self.in_pairs(value):
            seats = [self.seat(name, block) for name in EXPANDS]
            seat = jnp.where(which == 0, seats[0], jnp.where(which == 1, seats[1], seats[2]))
            at = pl.multiple_of(seat * part.shape[0], 16)
            self.s_expand[side, pl.ds(at, part.shape[0]), pl.ds(low, value.shape[1])] = part

    def put_reduce(self, step, side, low, value):
        count, piece = 32, self.s_reduce.shape[1] // 2
        eighth = piece // 8
        for n in range(value.shape[0] // count):
            row = step * value.shape[0] + n * count
            block, rest = lax.div(row, 2 * eighth), lax.rem(row, 2 * eighth)
            bits = {Z1: lax.div(block, 4), Y: lax.rem(lax.div(block, 2), 2), X: lax.rem(block, 2)}
            which, inside = lax.div(rest, eighth), lax.rem(rest, eighth)
            seats = []
            for name in REDUCES:
                a, b, c = (bits[link] for link in ORDER[name])
                seats.append(4 * a + 2 * b + c)
            at = which * piece + jnp.where(which == 0, *seats) * eighth + inside
            part = value[n * count : (n + 1) * count].astype(BF16)
            self.s_reduce[side, pl.ds(pl.multiple_of(at, 32), count), :] = part


    def vec_go(self, step):
        n = len(PIECES)
        source = self.v_half.at[1 - self.feat] if step == 0 else self.v_sum.at[step - 1]
        self.remote(
            source, self.v_land.at[step], self.send_sem.at[n, step], self.recv_sem.at[n, step], step
        ).start()

    def vec_step(self, step):
        n = len(PIECES)
        own = self.v_half.at[self.feat] if step == 0 else self.v_sum.at[step - 1]
        self.remote(
            own, self.v_land.at[step], self.send_sem.at[n, step], self.recv_sem.at[n, step], step
        ).wait()
        self.v_sum[step] = own[...] + self.v_land[step]
        if step < 4:
            self.vec_go(step + 1)


    def tick(self, name, step=None):
        for action, at in self.table.get(name, ()):
            if at is None or isinstance(step, int):
                if at is None or at == step:
                    self.act(action)
            else:
                pl.when(step == at)(functools.partial(self.act, action))

    def act(self, action):
        verb, name = action
        if verb == SEND:
            self.go(name, 0)
        elif verb == FREE:
            for other in name:
                self.travel(other, 0).wait_send()
                self.gone.add((other, 0))
            if name == MIDDLE:
                for other in INS:
                    self.allow(other, ORDER[other][0])
            else:
                for other in MIDDLE if name == REDUCES else (S_OUT, *INS):
                    self.allow(other, FEAT)
        elif verb == GO:
            self.go(name, 1)
        elif verb == BEGIN:
            for copy in self.copies_out(name):
                copy.start()
        elif verb == REUSE:
            near, far = self.copies_out(name)
            near.wait()
            far.wait_send()
        else:
            self.step(name, verb)

    def run(self):
        self.table, self.gone = {}, set()
        for name, at, actions in SCHEDULE:
            self.table.setdefault(name, []).extend((action, at) for action in actions)
        self.where_am_i()
        self.exchange()
        for copy in self.own:
            copy.start()
        self.start_weights()
        place = self.gs_half.at[self.feat]
        place[0:3, :] = self.gains[...]
        place[3:6, :] = self.shifts[...]
        self.greet()
        for copy in self.sent:
            copy.start()
        self.prepare()
        self.vec[...] = jnp.zeros(self.vec.shape, F32)
        self.landed(3)
        self.gs[...] = jnp.concatenate([self.gs_half[0], self.gs_half[1]], axis=1)
        self.landed(0)
        self.x[...] = self.x_t[...].T
        self.phases()
        self.act((BEGIN, INPUT_GRAD))
        self.v_half[0] = self.vec[:, : self.width // 2]
        self.v_half[1] = pltpu.roll(self.vec[...], self.width // 2, 1)[:, : self.width // 2]
        self.vec_go(0)
        for step in range(5):
            self.tick(END, step)
            self.vec_step(step)
        self.tick(END, 5)
        self.o_gain[...] = self.v_sum[4][0:3]
        self.o_shift[...] = self.v_sum[4][3:6]
        for name in PIECES:
            for step in range(5):
                if (name, step) not in self.gone:
                    self.travel(name, step).wait_send()
        for name in (LAYER_OUT, ENCODER_GRAD, INPUT_GRAD):
            if name != LAYER_OUT:
                self.act((REUSE, name))
            self.copies_out(name, local=False)[0].wait_recv()


def takes(step, *names):
    return tuple((step, name) for name in names)


SCHEDULE = (
    (FFN, 0, takes(SEND, EXPAND0)),
    (FFN, 1, takes(SEND, EXPAND1) + takes(0, EXPAND0)),
    (FFN, 2, takes(GO, EXPAND0) + takes(SEND, EXPAND2) + takes(0, EXPAND1)),
    (FFN_END, None, takes(SEND, REDUCE0, REDUCE1)),
    (NORM_3, 0, takes(GO, EXPAND1) + takes(0, EXPAND2, REDUCE0)),
    (NORM_3, 1, takes(GO, EXPAND2, REDUCE0) + takes(0, REDUCE1) + takes(BEGIN, LAYER_OUT)),
    (CROSS_START, None, takes(GO, REDUCE1) + takes(FREE, REDUCES, EXPANDS)),
    (MIXED, None, takes(SEND, S_MIX)),
    (KV, None, takes(SEND, S_KV) + takes(0, S_MIX) + takes(1, REDUCE0, REDUCE1) + takes(GO, S_MIX)),
    (NORM_2, 0, takes(0, S_KV)),
    (NORM_2, 1, takes(GO, S_KV) + takes(FREE, MIDDLE) + takes(BEGIN, ENCODER_GRAD) + takes(REUSE, LAYER_OUT)),
    (SELF_START, None, takes(SEND, S_OUT) + takes(1, *EXPANDS)),
    (SELF, 0, takes(0, S_OUT)),
    (SELF, 1, takes(GO, S_OUT)),
    (SELF, 3, takes(2, *REDUCES)),
    (IN, 0, takes(SEND, S_IN0)),
    (IN, 1, takes(SEND, S_IN1) + takes(0, S_IN0) + takes(GO, S_IN0)),
    (IN, 2, takes(SEND, S_IN2) + takes(0, S_IN1) + takes(GO, S_IN1)),
    (IN, 2, takes(0, S_IN2) + takes(GO, S_IN2) + takes(3, *REDUCES) + takes(2, *EXPANDS) + takes(1, S_MIX)),
    (NORM_1, 0, takes(1, S_KV, S_OUT)),
    (NORM_1, 1, takes(3, *EXPANDS) + takes(2, S_MIX)),
    (END, 1, takes(1, *INS)),
    (END, 2, takes(3, S_MIX) + takes(2, S_OUT, S_KV)),
    (END, 3, takes(2, *INS) + takes(4, *EXPANDS) + takes(4, *REDUCES)),
    (END, 4, takes(3, S_OUT, S_KV, *INS) + takes(4, S_MIX)),
    (END, 5, takes(4, S_OUT, S_KV, *INS)),
)


def spaces():
    return tuple(pl.BlockSpec(memory_space=s) for s in (pltpu.VMEM, pl.ANY, pltpu.SMEM))


def spill_outs(rows, hbm):
    return {
        f"spill{b}": (jax.ShapeDtypeStruct((HEADS, kn, qn), BF16), hbm)
        for b, (_, qn, _, kn) in enumerate(self_blocks(rows))
    }


COST = pl.CostEstimate(flops=50 * 10**9, bytes_accessed=40 * 10**6, transcendentals=0)


def local_layer(x, enc, og, t_len, s_len, gs, weights):
    rows, width = x.shape
    hidden = weights[5].shape[1]
    vmem, hbm, smem = spaces()
    shape = jax.ShapeDtypeStruct
    ins = dict(x=x, enc=enc, og=og, t_len=t_len, s_len=s_len, gs=gs)
    whole, pairs = shape((rows, width), F32), lambda n: (shape((2, width, n), BF16), hbm)
    outs = dict(
        layer_out=(whole, vmem),
        mid2=(whole, vmem),
        encoder_grad=(shape((rows, width), BF16), vmem),
        vec=(shape((8, width), F32), vmem),
        s_reduce=(shape((2, hidden // 2, width), BF16), vmem),
        s_expand=(shape((2, width, hidden // 2), BF16), vmem),
        to_kv=pairs(LANES[S_KV]),
        to_mix=pairs(LANES[S_MIX]),
        to_out=pairs(LANES[S_OUT]),
        to_in0=pairs(LANES[S_IN0]),
        to_in1=pairs(LANES[S_IN1]),
        to_in2=pairs(LANES[S_IN2]),
        **spill_outs(rows, hbm),
    )
    scratch = dict(scratch_of(rows, width, hidden), s_sem=pltpu.SemaphoreType.DMA((12,)))

    def kernel(*refs):
        first, rest = refs[: len(ins)], refs[len(ins) + 7 :]
        named = dict(zip(list(ins) + list(outs) + list(scratch), first + rest))
        LocalLayer(**share(sources=refs[len(ins) : len(ins) + 7], **named)).run()

    found = pl.pallas_call(
        kernel,
        out_shape=[o[0] for o in outs.values()],
        in_specs=[vmem, vmem, vmem, smem, smem, vmem] + [hbm] * 7,
        out_specs=[o[1] for o in outs.values()],
        scratch_shapes=list(scratch.values()),
        compiler_params=pltpu.CompilerParams(vmem_limit_bytes=VMEM_LIMIT),
        cost_estimate=COST,
    )(*ins.values(), *weights)
    return dict(zip(outs, found))


def whole_layer(inputs, encoder, output_grad, t_len, s_len, gains, shifts, weights):
    rows, half = inputs.shape[1] // 2, inputs.shape[0]
    width, hidden = 2 * half, weights[5].shape[1]
    shard = width // 16
    vmem, hbm, smem = spaces()
    shape = jax.ShapeDtypeStruct
    ins = dict(x_in=inputs, e_in=encoder, g_in=output_grad, t_len=t_len, s_len=s_len)
    ins.update(gains=gains, shifts=shifts)
    big, small = (shape(inputs.shape, F32), hbm), lambda *dims: (shape(dims, F32), vmem)
    outs = dict(
        layer_out=big,
        input_grad=big,
        encoder_grad=big,
        o_gain=small(3, half),
        o_shift=small(3, half),
        o_in=small(shard, 3 * half),
        o_out=small(shard, half),
        o_cq=small(shard, half),
        o_kv=small(shard, width),
        o_co=small(shard, half),
        o_expand=small(shard, hidden // 2),
        o_reduce=small(hidden // 16, half),
    )
    count = len(outs)
    outs.update(spill_outs(rows, hbm))
    vm, pieces = pltpu.VMEM, len(PIECES)
    dma, regular = pltpu.SemaphoreType.DMA, pltpu.SemaphoreType.REGULAR
    scratch = dict(
        scratch_of(rows, width, hidden),
        x=vm((rows, width), F32),
        gs=vm((8, width), F32),
        vec=vm((8, width), F32),
        mid2=vm((rows, width), F32),
        x_t=vm((width, rows), F32),
        grad_t=vm((width, rows), F32),
        e_t=vm((width, rows), BF16),
        gs_half=vm((2, 8, half), F32),
        s_reduce=vm((2, hidden // 2, width), BF16),
        s_expand=vm((2, width, hidden // 2), BF16),
        l_reduce=vm((hidden // 2, width), BF16),
        l_expand=vm((width, hidden // 2), BF16),
        v_half=vm((2, 8, half), F32),
        v_sum=vm((5, 8, half), F32),
        v_land=vm((5, 8, half), F32),
        in_own=dma((3,)),
        in_send=dma((4,)),
        in_recv=dma((4,)),
        out_own=dma((3,)),
        out_send=dma((3,)),
        out_recv=dma((3,)),
        send_sem=dma((pieces + 1, 5)),
        recv_sem=dma((pieces + 1, 5)),
        credit=regular((pieces, 4)),
    )
    ends = []
    for name in PIECES:
        dims = (shard, EXPAND_LANES if name in EXPANDS else LANES.get(name))
        dims = (hidden // 32, half) if name in REDUCES else dims
        ends += [vm(dims, F32), vm(dims, BF16), vm(dims, BF16)]

    def kernel(*refs):
        first, rest = refs[: len(ins)], refs[len(ins) + 7 :]
        names = list(ins) + list(outs) + list(scratch)
        last = rest[len(outs) + len(scratch) :]
        named = dict(zip(names, first + rest))
        named.update(z_keep=last[0::3], z_send=last[1::3], z_land=last[2::3])
        RemoteLayer(**share(sources=refs[len(ins) : len(ins) + 7], **named)).run()

    found = pl.pallas_call(
        kernel,
        out_shape=[o[0] for o in outs.values()],
        in_specs=[hbm, hbm, hbm, smem, smem, vmem, vmem] + [hbm] * 7,
        out_specs=[o[1] for o in outs.values()],
        scratch_shapes=list(scratch.values()) + ends,
        compiler_params=pltpu.CompilerParams(
            vmem_limit_bytes=VMEM_LIMIT, collective_id=0, has_side_effects=True
        ),
        cost_estimate=COST,
    )(*ins.values(), *weights)
    return found[:count]


def hand_over(*arrays):
    count = len(arrays)

    def kernel(*refs):
        sources, targets, middle = (refs[n * count : (n + 1) * count] for n in range(3))
        before, after = refs[-2], refs[-1]
        comes = [pltpu.make_async_copy(sources[n], middle[n], before.at[n]) for n in range(count)]
        goes = [pltpu.make_async_copy(middle[n], targets[n], after.at[n]) for n in range(count)]
        for copy in comes:
            copy.start()
        for come, go in zip(comes, goes):
            come.wait()
            go.start()
        for copy in goes:
            copy.wait()

    _, hbm, _ = spaces()
    sems = [pltpu.SemaphoreType.DMA((count,))] * 2
    return pl.pallas_call(
        kernel,
        out_shape=[jax.ShapeDtypeStruct(a.shape, a.dtype) for a in arrays],
        in_specs=[hbm] * count,
        out_specs=[hbm] * count,
        scratch_shapes=[pltpu.VMEM(a.shape, a.dtype) for a in arrays] + sems,
        compiler_params=pltpu.CompilerParams(vmem_limit_bytes=VMEM_LIMIT),
    )(*arrays)


def gather_rows(part):
    return lax.all_to_all(part, "feat", split_axis=0, concat_axis=1, tiled=True)


def spread_rows(part):
    return lax.all_to_all(part, "feat", split_axis=1, concat_axis=0, tiled=True)


def over_feat(staged):
    return lax.psum_scatter(staged, "feat", scatter_dimension=0, tiled=True)[0]


def over_dp(part):
    return lax.psum_scatter(part, "dp", scatter_dimension=0, tiled=True).astype(F32)


def by_collectives(
    inputs, encoder, output_grad, target_lengths, source_lengths, gains, shifts, *weights
):
    width = weights[1].shape[0]
    half = width // 2
    vectors = jnp.concatenate([gains, shifts, jnp.zeros_like(gains[:2])], axis=0)
    vectors = lax.all_gather(vectors, "feat", axis=1, tiled=True)
    got = local_layer(
        gather_rows(inputs),
        gather_rows(encoder),
        gather_rows(output_grad),
        target_lengths,
        source_lengths,
        vectors,
        weights,
    )
    first = lax.axis_index("feat") == 0
    vec = lax.psum(got["vec"], ("dp", "feat"))
    vec = jnp.where(first, vec[:, :half], vec[:, half:])
    red = over_feat(got["s_reduce"])
    reduce_grad = over_dp(jnp.concatenate([red[:, :half], red[:, half:]], axis=0))
    expand_grad = over_dp(over_feat(got["s_expand"]))
    kv_grad = over_dp(over_feat(got["to_kv"]))
    mix = over_dp(over_feat(got["to_mix"]))
    out_grad = over_dp(over_feat(got["to_out"]))[:, :half]
    parts = [got["to_in0"], got["to_in1"], got["to_in2"]]
    wide = over_dp(over_feat(jnp.concatenate(parts, axis=2)))
    low, high = wide[:, : 3 * half], jnp.concatenate([wide[:, 896:960], wide[:, :896]], axis=1)
    return (
        spread_rows(got["layer_out"]),
        spread_rows(got["mid2"]),
        spread_rows(got["encoder_grad"]).astype(F32),
        vec[:3],
        vec[3:6],
        jnp.where(first, low, high),
        out_grad,
        mix[:, half:],
        kv_grad,
        mix[:, :half],
        expand_grad,
        reduce_grad,
    )


def by_remote_copies(
    inputs, encoder, output_grad, target_lengths, source_lengths, gains, shifts, *weights
):
    got = whole_layer(
        inputs.T, encoder.T, output_grad.T, target_lengths, source_lengths, gains, shifts, weights
    )
    got = hand_over(*got)
    return tuple(part.T for part in got[:3]) + tuple(got[3:])


def solution(mesh):
    rows, both = P("dp", "feat"), P(("dp", "feat"), None)
    columns, whole = P(None, "feat"), P()
    small = mesh.shape["dp"] == 16 and mesh.shape["feat"] == 2
    return jax.shard_map(
        by_remote_copies if small else by_collectives,
        mesh=mesh,
        in_specs=(rows, rows, rows, both, both, columns, columns) + (whole,) * 7,
        out_specs=(rows, rows, rows, columns, columns) + (rows,) * 7,
        check_vma=False,
    )
```
